128 devices in a mesh: img: 8 (over z_lo, x), freq: 16 (over z_hi, y, core).
Axes of the slice: x: 4, y: 4, z: 4 (z_hi: 2, z_lo: 2; z = z_hi * 2 + z_lo), core: 2. Of those that a mesh axis runs over, the one named last changes fastest.
Arguments:
- images: bfloat16 [2, 12288, 32768], P(None, 'img', 'freq'), may hold values from -6 to 6
- references: bfloat16 [2, 896, 32768], P(None, 'img', 'freq'), may hold values from -6 to 6
- noise_weight: float32 [32768], P('freq'), may hold values from 0.005 to 0.05
- prior_orient: int32 [12288], P('img'), may hold values from 0 to 895
- segment_brick: int32 [16, 896, 16, 1], P('freq', 'img'), may hold values from 0 to 127; in each aligned block of 1792 rows (0 to 1791, 1792 to 3583, ..., all dimensions but the last counted through in order) at most 35 rows name the same one
- segment_row: int32 [16, 896, 16], P('freq', 'img'), may hold values from 0 to 1999
- segment_kernel: int32 [16, 896, 16], P('freq', 'img'), may hold values from 0 to 7
- kernel_taps: float32 [8, 4], replicated, may hold values from 0.1 to 1
Outputs:
- posterior: float32 [896, 12288], P('freq', 'img')
- volume: float32 [128, 2, 2000, 128], P(('img', 'freq'))
The draws below stay inside these ranges and needn't reach their ends.
Inputs may be any that keep to these rules, and one draw needn't show every extreme that they name: `segment_brick`: counted in aligned blocks of 1792 segments in the map's order, no brick is named more than 35 times within one block, a bound that some block reaches.
All inputs are finite; a program needn't handle non-finite values.
Results may differ from the reference program's by a relative error of at most 0.014.
Values may be sent and summed in bfloat16 or wider, within the bound.
A program may use at most 128 MiB of HBM per device.

```python
import math
import jax
import jax.numpy as jnp
import numpy as np
from jax import lax

F = 32768
ORI = 896
SEG = 128
TAPS = 4
NKER = 8
IMG_DEV = 1536
BROWS = 2000
NIMG = 12288
SEGQ = 16
SEG_DEV = 1792
BRICKS = 128
CAP = 35
N_IMG = 8
N_FREQ = 16


def previous_orient(key):
    return jax.random.randint(jax.random.fold_in(key, 11), (NIMG,), 0, ORI, dtype=jnp.int32)


def drawn_references(key):
    return jnp.clip(jax.random.normal(jax.random.fold_in(key, 23), (2, ORI, F), jnp.float32), -6.0, 6.0)


def draw_references(key, part):
    sampled = drawn_references(key)
    return sampled.astype(jnp.bfloat16)


def draw_images(key, part):
    sampled = jnp.clip(jax.random.normal(jax.random.fold_in(key, 41), (2, NIMG, F), jnp.float32), -6.0, 6.0)
    return sampled.astype(jnp.bfloat16)


def draw_prior_orient(key, part):
    return previous_orient(key)


def place_ends(entries, key, low, high):
    longest = entries.shape.index(max(entries.shape))
    spots = []
    for shift in (0, 1):
        where = [jax.random.randint(jax.random.fold_in(key, axis), (), 0, length) for axis, length in enumerate(entries.shape)]
        where[longest] = (where[longest] + shift) % entries.shape[longest]
        spots.append(tuple(where))
    return entries.at[spots[0]].set(low).at[spots[1]].set(high)


def shard_levels(rng, dims, cuts, smallest, largest):
    def one(dim, shards_of):
        heights = jax.random.uniform(jax.random.fold_in(jax.random.fold_in(rng, 6), dim), (shards_of,), jnp.float32, smallest / len(cuts), largest / len(cuts))
        return jnp.repeat(jnp.exp(heights), dims[dim] // shards_of).reshape((-1,) + (1,) * (len(dims) - dim - 1))

    loudness = one(*cuts[0])
    for cut in cuts[1:]:
        loudness = loudness * one(*cut)
    return loudness


def assign_block(stream_key, own, number, rows, number_of, top, bound, lean):
    sequence = jax.random.permutation(stream_key, number_of)
    heavy_load, common = shares(number_of, rows * top, bound, lean, True), shares(number_of, rows * top, bound, lean, False)
    places = jnp.arange(number_of)

    def named(tallies, rotation):
        used = int((tallies > 0).sum())
        fixed = max(1, used // 4)
        passed = fixed + (places - fixed + rotation * (used - fixed)) % max(1, number_of - fixed)
        return jnp.zeros((number_of,), jnp.int32).at[sequence[jnp.where(places < fixed, places, passed)]].set(jnp.asarray(tallies, jnp.int32))

    tallies = jnp.where(number % 4 == 0, named(heavy_load, number // 4), named(common, number - number // 4 - 1))
    mixed = jax.random.permutation(jax.random.fold_in(own, 3), number_of)
    giver, taker = mixed[0:number_of // 2 * 2:2], mixed[1:number_of // 2 * 2:2]
    slack = jnp.minimum(tallies[giver] - 1, bound - tallies[taker]) // 2
    slack = jnp.where((giver == sequence[0]) | (taker == sequence[0]) | (tallies[taker] == 0), 0, jnp.maximum(slack, 0))
    passed = jax.random.randint(jax.random.fold_in(own, 4), (number_of // 2,), 0, 1 << 20) % (slack + 1)
    tallies = tallies.at[giver].add(-passed).at[taker].add(passed)
    members = jnp.searchsorted(jnp.cumsum(tallies), jnp.arange(rows * top), side="right").astype(jnp.int32)
    table = members.reshape(top, rows).T
    table = table[jax.random.permutation(jax.random.fold_in(own, 1), rows)]
    rotation = jax.random.randint(jax.random.fold_in(own, 2), (rows, 1), 0, top)
    return jnp.take_along_axis(table, (jnp.arange(top)[None, :] + rotation) % top, axis=1)


def shares(number_of, total, limit, lean, full):
    loads = [(1 << 20) // math.isqrt(grade ** lean) + 1 for grade in range(1, number_of + 1)]
    largest = limit if full else min(limit, max(-(-total // number_of), total * loads[0] // sum(loads)))
    least = 1 if total - largest >= number_of - 1 else 0
    holding, rest = [largest] + [least] * (number_of - 1), total - largest - least * (number_of - 1)
    while rest > 0:
        free = [i for i in range(1, number_of) if holding[i] < largest] or [i for i in range(1, number_of) if holding[i] < limit]
        mass, remaining = sum([loads[i] for i in free]), rest
        for i in free:
            more = min(limit - holding[i], max(1, remaining * loads[i] // mass), rest)
            holding[i] = holding[i] + more
            rest = rest - more
    return np.array(holding)


def setup_inputs(seed: int = 0) -> dict:
    splits = jax.random.split(jax.random.key(seed), 9)
    images = draw_images(jax.random.fold_in(splits[8], 71), 0)
    references = draw_references(jax.random.fold_in(splits[8], 71), 0)
    noise_weight = jnp.clip(jnp.exp(math.log(0.05) - 2.3025851 * jax.random.uniform(splits[2], (F,), jnp.float32) ** shard_levels(splits[2], (F,), ((0, 16),), -0.2, 0.2)), 0.005, 0.05)
    prior_orient = draw_prior_orient(jax.random.fold_in(splits[8], 71), 0)
    segment_brick_keys = jax.random.split(jax.random.fold_in(splits[4], 1), N_FREQ * ORI * SEGQ // SEG_DEV)
    segment_brick_turns = jax.random.permutation(jax.random.fold_in(splits[4], 3), N_FREQ * ORI * SEGQ // SEG_DEV)
    segment_brick = jax.vmap(lambda own, number: assign_block(jax.random.fold_in(splits[4], 2), own, number, SEG_DEV, BRICKS, 1, CAP, 1))(segment_brick_keys, segment_brick_turns).reshape((N_FREQ, ORI, SEGQ, 1))
    segment_row = place_ends(jax.random.randint(splits[5], (N_FREQ, ORI, SEGQ), 0, BROWS), jax.random.fold_in(splits[5], 1), 0, BROWS - 1).astype(jnp.int32)
    segment_kernel = place_ends(jax.random.randint(splits[6], (N_FREQ, ORI, SEGQ), 0, NKER), jax.random.fold_in(splits[6], 1), 0, NKER - 1).astype(jnp.int32)
    kernel_taps = jnp.clip(jax.random.uniform(splits[7], (NKER, TAPS), jnp.float32, 0.1, 1.0), 0.1, 1.0)
    return {"images": images, "references": references, "noise_weight": noise_weight, "prior_orient": prior_orient, "segment_brick": segment_brick, "segment_row": segment_row, "segment_kernel": segment_kernel, "kernel_taps": kernel_taps}


tempering = 0.5
masked_logit = -1.0e30
contract_last = (((1,), (1,)), ((), ()))


def spread_taps(values, kernels, kernel_taps):
    phases = kernel_taps.shape[0]
    tap_count = kernel_taps.shape[1]
    member = (kernels[:, None] == jnp.arange(phases, dtype=jnp.int32)[None, :]).astype(kernel_taps.dtype)
    factors = jnp.dot(member, kernel_taps, precision=lax.Precision.HIGHEST)
    padded = jnp.pad(values, ((0, 0), (0, 0), (tap_count - 2, 1)))
    lane_count = values.shape[2]
    result = jnp.zeros(values.shape, values.dtype)
    for tap_index in range(tap_count):
        first_lane = tap_count - 1 - tap_index
        result = result + factors[:, tap_index, None, None] * padded[:, :, first_lane:first_lane + lane_count]
    return result


def window_logits(scores, orient_index, prior_orient, orient_count):
    distance = (orient_index[:, None] - prior_orient[None, :]) % orient_count
    half_window = orient_count // 8
    allowed = (distance <= half_window) | (distance >= orient_count - half_window)
    return jnp.where(allowed, tempering * scores, masked_logit)


def reference(images, references, noise_weight, prior_orient, segment_brick, segment_row, segment_kernel, kernel_taps):
    unpacked = references.astype(jnp.float32)
    weighted = (noise_weight * unpacked).astype(jnp.bfloat16)
    energies = jnp.sum(noise_weight * (unpacked[0] * unpacked[0] + unpacked[1] * unpacked[1]), axis=1)
    products = lax.dot_general(weighted[0], images[0], contract_last, preferred_element_type=jnp.float32)
    products = products + lax.dot_general(weighted[1], images[1], contract_last, preferred_element_type=jnp.float32)
    scores = products - 0.5 * energies[:, None]
    orient_index = jnp.arange(ORI, dtype=jnp.int32)
    logits = window_logits(scores, orient_index, prior_orient, ORI)
    highest = jnp.max(logits, axis=0)
    raised = jnp.exp(logits - highest[None, :])
    posterior = raised / jnp.sum(raised, axis=0)[None, :]
    rounded = posterior.astype(jnp.bfloat16)

    def add_group(group_index, running):
        first_image = jnp.asarray(group_index, jnp.int32) * IMG_DEV
        weights = lax.dynamic_slice_in_dim(rounded, first_image, IMG_DEV, 1)
        image_block = lax.dynamic_slice_in_dim(images, first_image, IMG_DEV, 1)
        partial_value = jnp.stack((jnp.dot(weights, image_block[0], preferred_element_type=jnp.float32),
                             jnp.dot(weights, image_block[1], preferred_element_type=jnp.float32)), axis=1)
        narrowed = lax.optimization_barrier(partial_value.astype(jnp.bfloat16))
        return running + narrowed.astype(jnp.float32)

    weighted_sums = lax.fori_loop(0, N_IMG, add_group, jnp.zeros((ORI, 2, F), jnp.float32))
    segment_blocks = F // N_FREQ // SEG
    values = weighted_sums.reshape(ORI, 2, N_FREQ, segment_blocks, SEG).transpose(2, 0, 3, 1, 4).reshape(-1, 2, SEG)
    contributions = spread_taps(values, segment_kernel.reshape(-1), kernel_taps)
    places = segment_brick.reshape(-1) * BROWS + segment_row.reshape(-1)
    volume = jnp.zeros((BRICKS * BROWS, 2, SEG), jnp.float32).at[places].add(contributions)
    volume = volume.reshape(BRICKS, BROWS, 2, SEG).transpose(0, 2, 1, 3)
    return posterior, volume
```

```python
import jax
import jax.numpy as jnp
from jax import lax
from jax.sharding import PartitionSpec as P

BROWS = 2000
KEPT = 240
COARSE = 128
FINE = (64, 32, 16, 8)


tempering = 0.5
masked_logit = -1e30
contract_last = (((1,), (1,)), ((), ()))


def window_parts(prior_orient, orient_count):
    start = (prior_orient - orient_count // 8) % orient_count
    return start // COARSE, start % COARSE


def to_windows(scores, prior_orient):
    orient_count = scores.shape[0]
    coarse, fine = window_parts(prior_orient, orient_count)
    rows = KEPT + sum(FINE)
    ring = jnp.concatenate([scores, scores[: rows - COARSE]], axis=0)
    kept = ring[:rows]
    for block in range(1, orient_count // COARSE):
        kept = jnp.where((coarse == block)[None], ring[block * COARSE : block * COARSE + rows], kept)
    for step in FINE:
        rows -= step
        kept = jnp.where(((fine // step) % 2 == 1)[None], kept[step : step + rows], kept[:rows])
    return kept


def from_windows(kept, prior_orient, orient_count):
    coarse, fine = window_parts(prior_orient, orient_count)
    for step in FINE[::-1]:
        pad = jnp.zeros((step, kept.shape[1]), kept.dtype)
        kept = jnp.where(
            ((fine // step) % 2 == 1)[None],
            jnp.concatenate([pad, kept], axis=0),
            jnp.concatenate([kept, pad], axis=0),
        )
    kept = jnp.pad(kept, ((0, -kept.shape[0] % COARSE), (0, 0)))
    blocks = orient_count // COARSE
    parts = []
    for block in range(blocks):
        part = jnp.zeros((COARSE, kept.shape[1]), kept.dtype)
        for piece in range(kept.shape[0] // COARSE):
            part = jnp.where(
                (coarse == (block - piece) % blocks)[None],
                kept[piece * COARSE : (piece + 1) * COARSE],
                part,
            )
        parts.append(part)
    return jnp.concatenate(parts, axis=0)


def window_softmax(scores, prior_orient, orient_count):
    fine = window_parts(prior_orient, orient_count)[1] % FINE[-1]
    position = jnp.arange(scores.shape[1], dtype=jnp.int32)[None, :]
    inside = (position >= fine[:, None]) & (position <= fine[:, None] + 2 * (orient_count // 8))
    logits = jnp.where(inside, tempering * scores, masked_logit)
    raised = jnp.where(inside, jnp.exp(logits - jnp.max(logits, axis=1, keepdims=True)), 0.0)
    return raised / jnp.sum(raised, axis=1, keepdims=True)


def spread_taps(values, kernels, kernel_taps):
    phases, tap_count = kernel_taps.shape
    member = (kernels[:, None] == jnp.arange(phases, dtype=jnp.int32)[None, :]).astype(
        kernel_taps.dtype
    )
    factors = jnp.dot(member, kernel_taps, precision=lax.Precision.HIGHEST)
    padded = jnp.pad(values, ((0, 0), (0, 0), (tap_count - 2, 1)))
    lane_count = values.shape[2]
    result = jnp.zeros(values.shape, values.dtype)
    for tap_index in range(tap_count):
        first_lane = tap_count - 1 - tap_index
        result = (
            result
            + factors[None, :, tap_index, None] * padded[:, :, first_lane : first_lane + lane_count]
        )
    return result


def on_device(
    images,
    references,
    noise_weight,
    prior_orient,
    segment_brick,
    segment_row,
    segment_kernel,
    kernel_taps,
):
    image_groups = lax.axis_size("img")
    freq_groups = lax.axis_size("freq")
    local_orients = references.shape[1]
    orient_count = local_orients * image_groups
    share_rows = orient_count // freq_groups
    share_images = images.shape[1] // freq_groups
    unpacked = lax.all_gather(references, "img", axis=1, tiled=True).astype(jnp.float32)
    weighted = (noise_weight * unpacked).astype(jnp.bfloat16)
    energies = jnp.sum(
        noise_weight * (unpacked[0] * unpacked[0] + unpacked[1] * unpacked[1]), axis=1
    )
    products = lax.dot_general(
        weighted[0], images[0], contract_last, preferred_element_type=jnp.float32
    )
    products = products + lax.dot_general(
        weighted[1], images[1], contract_last, preferred_element_type=jnp.float32
    )
    partial_scores = products - 0.5 * energies[:, None]
    windows = to_windows(partial_scores, prior_orient).T
    scores = lax.psum_scatter(windows, "freq", scatter_dimension=0, tiled=True)
    own_prior = lax.dynamic_slice_in_dim(
        prior_orient, lax.axis_index("freq") * share_images, share_images, 0
    )
    kept = window_softmax(scores, own_prior, orient_count).astype(jnp.bfloat16)
    kept = lax.all_gather(kept, "freq", axis=0, tiled=True).T
    rounded = from_windows(kept, prior_orient, orient_count)
    own_rows = lax.dynamic_slice_in_dim(
        rounded, lax.axis_index("freq") * share_rows, share_rows, 0
    ).astype(jnp.float32)
    weighted_sums = lax.psum_scatter(
        jnp.einsum("oi,cif->cof", rounded, images, preferred_element_type=jnp.float32).astype(
            jnp.bfloat16
        ),
        "img",
        scatter_dimension=1,
        tiled=True,
    ).astype(jnp.float32)
    segment_blocks = segment_row.shape[2]
    lane_count = images.shape[2] // segment_blocks
    local_segments = local_orients * segment_blocks
    values = weighted_sums.reshape(2, local_orients, segment_blocks, lane_count)
    values = values.transpose(0, 2, 1, 3).reshape(2, local_segments, lane_count)
    targets = segment_brick.reshape(local_orients, segment_blocks).T.reshape(-1)
    voxel_rows = segment_row.reshape(local_orients, segment_blocks).T.reshape(-1)
    kernels = segment_kernel.reshape(local_orients, segment_blocks).T.reshape(-1)
    brick_count = image_groups * freq_groups
    capacity = max(2, 5 * local_segments // (2 * brick_count))
    segment_ids = jnp.arange(local_segments, dtype=jnp.int32)
    same_brick = (targets[:, None] == targets[None, :]) & (
        segment_ids[None, :] < segment_ids[:, None]
    )
    rank_within = jnp.sum(same_brick.astype(jnp.int32), axis=1)
    places = targets * capacity + rank_within
    slot_total = brick_count * capacity
    slot_ids = jnp.arange(slot_total, dtype=jnp.int32)
    slot_hits = places[None, :] == slot_ids[:, None]
    packed_rows = jnp.sum(jnp.where(slot_hits, voxel_rows[None, :], 0), axis=1)
    contributions = spread_taps(values, kernels, kernel_taps).astype(jnp.bfloat16)
    hits = slot_hits.astype(jnp.bfloat16)
    packed = jnp.stack(
        [jnp.dot(hits, part, preferred_element_type=jnp.float32) for part in contributions], axis=1
    ).astype(jnp.bfloat16)
    exchange = lambda lines: lax.all_to_all(
        lines.reshape(brick_count, capacity, -1),
        ("img", "freq"),
        split_axis=0,
        concat_axis=0,
        tiled=True,
    )
    arrived_rows = exchange(packed_rows).reshape(-1)
    arrived = exchange(packed).reshape(slot_total, 2 * lane_count)
    row_member = arrived_rows[None, :] == jnp.arange(BROWS, dtype=jnp.int32)[:, None]
    volume = jnp.stack(
        [
            jnp.dot(
                row_member.astype(jnp.bfloat16),
                arrived[:, part * lane_count : (part + 1) * lane_count],
                preferred_element_type=jnp.float32,
            )
            for part in range(2)
        ]
    )
    return (own_rows, volume[None])


def solution(mesh):
    in_specs = (
        P(None, "img", "freq"),
        P(None, "img", "freq"),
        P("freq"),
        P("img"),
        P("freq", "img", None, None),
        P("freq", "img", None),
        P("freq", "img", None),
        P(),
    )
    out_specs = (P("freq", "img"), P(("img", "freq"), None, None, None))
    return jax.shard_map(
        on_device, mesh=mesh, in_specs=in_specs, out_specs=out_specs, check_vma=False
    )
```

```python
import jax
import jax.numpy as jnp
from jax import lax
from jax.experimental import pallas as pl
from jax.experimental.pallas import tpu as pltpu
from jax.sharding import PartitionSpec as P

MESH = pl.DeviceIdType.MESH
VMEM = pltpu.VMEM
DMA = pltpu.SemaphoreType.DMA
VMEM_BYTES = 60 * 1024 * 1024
RING = 4

BROWS = 2000
KEPT = 256
COARSE = 128
FINE = (64, 32, 16, 8)


tempering = 0.5
masked_logit = -1e30
contract_last = (((1,), (1,)), ((), ()))


def window_parts(prior_orient, orient_count):
    start = (prior_orient - orient_count // 8) % orient_count
    return start // COARSE, start % COARSE


def to_windows(scores, prior_orient):
    orient_count = scores.shape[0]
    coarse, fine = window_parts(prior_orient, orient_count)
    rows = KEPT + sum(FINE)
    ring = jnp.concatenate([scores, scores[: rows - COARSE]], axis=0)
    kept = ring[:rows]
    for block in range(1, orient_count // COARSE):
        kept = jnp.where((coarse == block)[None], ring[block * COARSE : block * COARSE + rows], kept)
    for step in FINE:
        rows -= step
        kept = jnp.where(((fine // step) % 2 == 1)[None], kept[step : step + rows], kept[:rows])
    return kept


def from_windows(kept, prior_orient, orient_count):
    coarse, fine = window_parts(prior_orient, orient_count)
    for step in FINE[::-1]:
        pad = jnp.zeros((step, kept.shape[1]), kept.dtype)
        kept = jnp.where(
            ((fine // step) % 2 == 1)[None],
            jnp.concatenate([pad, kept], axis=0),
            jnp.concatenate([kept, pad], axis=0),
        )
    kept = jnp.pad(kept, ((0, -kept.shape[0] % COARSE), (0, 0)))
    blocks = orient_count // COARSE
    parts = []
    for block in range(blocks):
        part = jnp.zeros((COARSE, kept.shape[1]), kept.dtype)
        for piece in range(kept.shape[0] // COARSE):
            part = jnp.where(
                (coarse == (block - piece) % blocks)[None],
                kept[piece * COARSE : (piece + 1) * COARSE],
                part,
            )
        parts.append(part)
    return jnp.concatenate(parts, axis=0)


def img_neighbours():
    me = lax.axis_index("img")
    z, x = me // RING, me % RING
    at = lambda other, shift: (z + other) % 2 * RING + (x + shift) % RING
    return at


def greet(axis, others):
    barrier = pltpu.get_barrier_semaphore()
    for other in others:
        pl.semaphore_signal(barrier, inc=1, device_id={axis: other}, device_id_type=MESH)
    pl.semaphore_wait(barrier, len(others))


def score_kernel(
    refs_ref, noise_ref, images_hbm, out_ref, images, gathered, weighted, energy,
    load_sem, own_sem, send_sem, recv_sem,
):
    at = img_neighbours()
    rows = refs_ref.shape[1]
    load = pltpu.make_async_copy(images_hbm, images, load_sem)
    load.start()
    own = pltpu.make_async_copy(refs_ref, gathered.at[at(0, 0)], own_sem)
    own.start()
    greet("img", [at(0, 1), at(0, 3), at(1, 0)])
    own.wait()

    def send(number, shard, part, target):
        copy = pltpu.make_async_remote_copy(
            src_ref=gathered.at[shard, part],
            dst_ref=gathered.at[shard, part],
            send_sem=send_sem.at[number],
            recv_sem=recv_sem.at[number],
            device_id={"img": target},
            device_id_type=MESH,
        )
        copy.start()
        return copy

    right, left, across = at(0, 1), at(0, 3), at(1, 0)
    mine = at(0, 0)
    own_right = [send(0, mine, 0, right), None]
    own_left = [None, send(1, mine, 1, left)]
    own_across = [send(2, mine, 0, across), None]
    own_right[1] = send(3, mine, 1, right)
    own_left[0] = send(4, mine, 0, left)
    own_across[1] = send(5, mine, 1, across)

    def weigh(shard, part, place, fresh):
        lines = 16

        def body(step, _):
            at_row = pl.multiple_of(step * lines, lines)
            value = gathered[shard, part, pl.ds(at_row, lines), :].astype(jnp.float32)
            scaled = value * noise_ref[...]
            weighted[pl.ds(pl.multiple_of(place * rows + at_row, lines), lines), :] = scaled.astype(
                jnp.bfloat16
            )
            total = jnp.sum(scaled * value, axis=1, keepdims=True)
            here = pl.ds(pl.multiple_of(place * rows + at_row, lines), lines)
            if fresh:
                energy[here, :] = jnp.broadcast_to(total, (lines, 128))
            else:
                energy[here, :] = energy[here, :] + total
            return 0

        lax.fori_loop(0, rows // lines, body, 0)

    def multiply(first, second, part, fresh):
        weigh(first, part, 0, fresh)
        weigh(second, part, 1, fresh)
        width = 256

        def body(step, _):
            column = pl.ds(pl.multiple_of(step * width, width), width)
            product = lax.dot_general(
                weighted[...], images[part, column, :], contract_last,
                preferred_element_type=jnp.float32,
            )
            if not fresh:
                product = product - 0.5 * jnp.tile(energy[...], (1, width // 128))
            for place, shard in enumerate((first, second)):
                block = product[place * rows : (place + 1) * rows]
                there = pl.ds(pl.multiple_of(shard * rows, 16), rows)
                if fresh:
                    out_ref[there, column] = block
                else:
                    out_ref[there, column] = out_ref[there, column] + block
            return 0

        lax.fori_loop(0, images.shape[1] // width, body, 0)

    own_right[0].wait_recv()
    next_right = send(6, at(0, 3), 0, right)
    own_left[1].wait_recv()
    next_left = send(7, at(0, 1), 1, left)
    load.wait()
    own_across[0].wait_recv()
    over_right = [send(8, at(1, 0), 0, right), None]
    over_left = [send(9, at(1, 0), 0, left), None]
    multiply(at(0, 0), at(1, 0), 0, True)
    own_across[1].wait_recv()
    over_right[1] = send(10, at(1, 0), 1, right)
    over_left[1] = send(11, at(1, 0), 1, left)
    multiply(at(0, 0), at(1, 0), 1, False)
    own_right[1].wait_recv()
    own_left[0].wait_recv()
    next_right.wait_recv()
    over_across = [send(12, at(0, 2), 0, across), None]
    next_left.wait_recv()
    over_across[1] = send(13, at(0, 2), 1, across)
    multiply(at(0, 1), at(0, 3), 0, True)
    multiply(at(0, 1), at(0, 3), 1, False)
    over_right[0].wait_recv()
    over_left[0].wait_recv()
    multiply(at(1, 1), at(1, 3), 0, True)
    over_right[1].wait_recv()
    over_left[1].wait_recv()
    multiply(at(1, 1), at(1, 3), 1, False)
    over_across[0].wait_recv()
    multiply(at(0, 2), at(1, 2), 0, True)
    over_across[1].wait_recv()
    multiply(at(0, 2), at(1, 2), 1, False)
    for copy in (
        own_right + own_left + own_across + [next_right, next_left]
        + over_right + over_left + over_across
    ):
        copy.wait_send()


def gathered_scores(references, noise_weight, images, image_groups):
    parts, rows, freqs = references.shape
    count = images.shape[1]
    return pl.pallas_call(
        score_kernel,
        out_shape=jax.ShapeDtypeStruct((image_groups * rows, count), jnp.float32),
        in_specs=[pl.BlockSpec(memory_space=VMEM)] * 2 + [pl.BlockSpec(memory_space=pl.ANY)],
        out_specs=pl.BlockSpec(memory_space=VMEM),
        scratch_shapes=[
            VMEM(images.shape, jnp.bfloat16),
            VMEM((image_groups, parts, rows, freqs), jnp.bfloat16),
            VMEM((2 * rows, freqs), jnp.bfloat16),
            VMEM((2 * rows, 128), jnp.float32),
            DMA(()),
            DMA(()),
            DMA((14,)),
            DMA((14,)),
        ],
        compiler_params=pltpu.CompilerParams(
            collective_id=0, has_side_effects=True, vmem_limit_bytes=VMEM_BYTES
        ),
    )(references, noise_weight.reshape(1, freqs), images)


def posterior_kernel(
    windows_ref, fine_ref, out_ref, pair_in, chip_out, chip_in,
    pair_send, pair_recv, chip_send, chip_recv, gat_send, gat_recv, sib_send, sib_recv,
):
    me = lax.axis_index("freq")
    core = me % 2
    z, y = me // 8, me // 2 % 4
    count = windows_ref.shape[0] // 16
    sibling = me + 1 - 2 * core
    spots = [(dz, dy) for dz, dy in ((1, 2), (1, 1), (1, 3), (0, 2), (1, 0), (0, 1), (0, 3), (0, 0))]
    target = lambda dz, dy: (z + dz) % 2 * 8 + (y + dy) % 4 * 2 + core
    source = lambda dz, dy: (z + dz) % 2 * 8 + (y + 4 - dy) % 4 * 2 + core
    greet("freq", [target(*spot) for spot in spots[:-1]] + [sibling])
    lines = lambda block: pl.ds(pl.multiple_of(block * count, 16), count)

    def send(src, dst, send_sem, recv_sem, other):
        copy = pltpu.make_async_remote_copy(
            src_ref=src, dst_ref=dst, send_sem=send_sem, recv_sem=recv_sem,
            device_id={"freq": other}, device_id_type=MESH,
        )
        copy.start()
        return copy

    pairs = []
    for n, spot in enumerate(spots):
        block = target(*spot) + 1 - 2 * core
        pairs.append(
            send(windows_ref.at[lines(block)], pair_in.at[n], pair_send.at[n], pair_recv.at[n], sibling)
        )
    chips = []
    for n, spot in enumerate(spots):
        pairs[n].wait_recv()
        total = windows_ref[lines(target(*spot)), :] + pair_in[n]
        if n == 7:
            break
        chip_out[n] = total
        chips.append(
            send(chip_out.at[n], chip_in.at[n], chip_send.at[n], chip_recv.at[n], target(*spot))
        )
    chip_out[7] = total
    scores = chip_out[7]
    for n in range(7):
        chips[6 - n].wait_recv()
        scores = scores + chip_in[6 - n]
    fine = fine_ref[...]
    position = lax.broadcasted_iota(jnp.int32, scores.shape, 1)
    inside = (position >= fine) & (position <= fine + 224)
    logits = jnp.where(inside, tempering * scores, masked_logit)
    raised = jnp.where(inside, jnp.exp(logits - jnp.max(logits, axis=1, keepdims=True)), 0.0)
    result = raised / jnp.sum(raised, axis=1, keepdims=True)
    out_ref[lines(me), :] = result.astype(jnp.bfloat16)
    gathers, relays = [], []
    for n, spot in enumerate(spots[:-1]):
        here = out_ref.at[lines(me)]
        gathers.append(send(here, here, gat_send.at[n], gat_recv.at[n], target(*spot)))
    here = out_ref.at[lines(me)]
    relays.append(send(here, here, sib_send.at[7], sib_recv.at[7], sibling))
    for n in range(6, -1, -1):
        gathers[n].wait_recv()
        here = out_ref.at[lines(source(*spots[n]))]
        relays.append(send(here, here, sib_send.at[n], sib_recv.at[n], sibling))
    for copy in relays:
        copy.wait_recv()
    for copy in pairs + chips + gathers + relays:
        copy.wait_send()


def windowed_posterior(windows, own_fine):
    rows, width = windows.shape
    count = rows // 16
    sems = [DMA((8,)) for _ in range(8)]
    return pl.pallas_call(
        posterior_kernel,
        out_shape=jax.ShapeDtypeStruct((rows, width), jnp.bfloat16),
        in_specs=[pl.BlockSpec(memory_space=VMEM)] * 2,
        out_specs=pl.BlockSpec(memory_space=VMEM),
        scratch_shapes=[VMEM((8, count, width), jnp.float32) for _ in range(3)] + sems,
        compiler_params=pltpu.CompilerParams(
            collective_id=1, has_side_effects=True, vmem_limit_bytes=VMEM_BYTES
        ),
    )(windows, own_fine)


def sums_kernel(
    rounded_ref, images_hbm, out_ref, images, lhs, part, first_in, side_in, half_in, near_in,
    last_in, load_sem, send_sem, recv_sem,
):
    at = img_neighbours()
    rows, freqs = out_ref.shape[1:]
    loads = []
    for n in range(2):
        loads.append(pltpu.make_async_copy(images_hbm.at[n], images.at[n], load_sem.at[n]))
        loads[-1].start()
    right, left, across = at(0, 1), at(0, 3), at(1, 0)
    greet("img", [right, left, across])

    def multiply(first, second, n):
        for place, (other, shift) in enumerate((first, second)):
            there = pl.ds(pl.multiple_of(at(other, shift) * rows, 16), rows)
            lhs[place * rows : (place + 1) * rows, :] = rounded_ref[there, :]
        width = 256

        def body(step, _):
            column = pl.ds(pl.multiple_of(step * width, width), width)
            product = jnp.dot(
                lhs[...], images[n, :, column], preferred_element_type=jnp.float32
            ).astype(jnp.bfloat16)
            for place, (other, shift) in enumerate((first, second)):
                part[other * 4 + shift, n, :, column] = product[place * rows : (place + 1) * rows]
            return 0

        lax.fori_loop(0, freqs // width, body, 0)

    copies = []

    def send(src, dst, target):
        number = len(copies)
        copy = pltpu.make_async_remote_copy(
            src_ref=src, dst_ref=dst, send_sem=send_sem.at[number], recv_sem=recv_sem.at[number],
            device_id={"img": target}, device_id_type=MESH,
        )
        copy.start()
        copies.append(copy)
        return copy

    def combine(dst, sources):
        lines = 16

        def body(step, _):
            here = pl.ds(pl.multiple_of(step * lines, lines), lines)
            total = sources[0][here, :].astype(jnp.float32)
            for source in sources[1:]:
                total = total + source[here, :].astype(jnp.float32)
            dst[here, :] = total.astype(dst.dtype)
            return 0

        lax.fori_loop(0, rows // lines, body, 0)

    first, sides, near = [], [[], []], [[None, None], [None, None]]
    for n in range(2):
        loads[n].wait()
        multiply((1, 2), (0, 2), n)
        first.append(send(part.at[6, n], first_in.at[n], across))
    for n in range(2):
        multiply((1, 1), (1, 3), n)
        sides[0].append(send(part.at[5, n], side_in.at[0, n], right))
        sides[1].append(send(part.at[7, n], side_in.at[1, n], left))
    for n in range(2):
        multiply((0, 1), (0, 3), n)
    halves = []
    first[0].wait_recv()
    combine(part.at[2, 0], [part.at[2, 0], first_in.at[0]])
    halves.append(send(part.at[2, 0], half_in.at[0], left))
    for n in range(2):
        multiply((1, 0), (0, 0), n)
    first[1].wait_recv()
    combine(part.at[2, 1], [part.at[2, 1], first_in.at[1]])
    halves.append(send(part.at[2, 1], half_in.at[1], right))
    near[0][0] = send(part.at[1, 0], near_in.at[0, 0], right)
    near[1][1] = send(part.at[3, 1], near_in.at[1, 1], left)
    last = []
    for n in range(2):
        sides[0][n].wait_recv()
        sides[1][n].wait_recv()
        combine(part.at[4, n], [part.at[4, n], side_in.at[0, n], side_in.at[1, n]])
        last.append(send(part.at[4, n], last_in.at[n], across))
    halves[0].wait_recv()
    combine(part.at[3, 0], [part.at[3, 0], half_in.at[0]])
    near[1][0] = send(part.at[3, 0], near_in.at[1, 0], left)
    halves[1].wait_recv()
    combine(part.at[1, 1], [part.at[1, 1], half_in.at[1]])
    near[0][1] = send(part.at[1, 1], near_in.at[0, 1], right)
    for n in range(2):
        near[0][n].wait_recv()
        near[1][n].wait_recv()
        last[n].wait_recv()
        combine(
            out_ref.at[n], [part.at[0, n], near_in.at[0, n], near_in.at[1, n], last_in.at[n]]
        )
    for copy in copies:
        copy.wait_send()


def scattered_sums(rounded, images, image_groups):
    rows = rounded.shape[0] // image_groups
    parts, count, freqs = images.shape
    block = (parts, rows, freqs)
    return pl.pallas_call(
        sums_kernel,
        out_shape=jax.ShapeDtypeStruct(block, jnp.float32),
        in_specs=[pl.BlockSpec(memory_space=VMEM), pl.BlockSpec(memory_space=pl.ANY)],
        out_specs=pl.BlockSpec(memory_space=VMEM),
        scratch_shapes=[
            VMEM(images.shape, jnp.bfloat16),
            VMEM((2 * rows, count), jnp.bfloat16),
            VMEM((image_groups, *block), jnp.bfloat16),
            VMEM(block, jnp.bfloat16),
            VMEM((2, *block), jnp.bfloat16),
            VMEM(block, jnp.bfloat16),
            VMEM((2, *block), jnp.bfloat16),
            VMEM(block, jnp.bfloat16),
            DMA((2,)),
            DMA((14,)),
            DMA((14,)),
        ],
        compiler_params=pltpu.CompilerParams(
            collective_id=2, has_side_effects=True, vmem_limit_bytes=VMEM_BYTES
        ),
    )(rounded, images)


def spread_taps(values, kernels, kernel_taps):
    phases, tap_count = kernel_taps.shape
    member = (kernels[:, None] == jnp.arange(phases, dtype=jnp.int32)[None, :]).astype(
        kernel_taps.dtype
    )
    factors = jnp.dot(member, kernel_taps, precision=lax.Precision.HIGHEST)
    padded = jnp.pad(values, ((0, 0), (0, 0), (tap_count - 2, 1)))
    lane_count = values.shape[2]
    result = jnp.zeros(values.shape, values.dtype)
    for tap_index in range(tap_count):
        first_lane = tap_count - 1 - tap_index
        result = (
            result
            + factors[None, :, tap_index, None] * padded[:, :, first_lane : first_lane + lane_count]
        )
    return result


def on_device(
    images,
    references,
    noise_weight,
    prior_orient,
    segment_brick,
    segment_row,
    segment_kernel,
    kernel_taps,
):
    image_groups = lax.axis_size("img")
    freq_groups = lax.axis_size("freq")
    local_orients = references.shape[1]
    orient_count = local_orients * image_groups
    share_rows = orient_count // freq_groups
    share_images = images.shape[1] // freq_groups
    partial_scores = gathered_scores(references, noise_weight, images, image_groups)
    windows = to_windows(partial_scores, prior_orient).T
    own_prior = lax.dynamic_slice_in_dim(
        prior_orient, lax.axis_index("freq") * share_images, share_images, 0
    )
    own_fine = window_parts(own_prior, orient_count)[1] % FINE[-1]
    kept = windowed_posterior(windows, own_fine[:, None]).T
    rounded = from_windows(kept, prior_orient, orient_count)
    own_rows = lax.dynamic_slice_in_dim(
        rounded, lax.axis_index("freq") * share_rows, share_rows, 0
    ).astype(jnp.float32)
    weighted_sums = scattered_sums(rounded, images, image_groups)
    segment_blocks = segment_row.shape[2]
    lane_count = images.shape[2] // segment_blocks
    local_segments = local_orients * segment_blocks
    values = weighted_sums.reshape(2, local_orients, segment_blocks, lane_count)
    values = values.transpose(0, 2, 1, 3).reshape(2, local_segments, lane_count)
    targets = segment_brick.reshape(local_orients, segment_blocks).T.reshape(-1)
    voxel_rows = segment_row.reshape(local_orients, segment_blocks).T.reshape(-1)
    kernels = segment_kernel.reshape(local_orients, segment_blocks).T.reshape(-1)
    brick_count = image_groups * freq_groups
    capacity = max(2, 5 * local_segments // (2 * brick_count))
    segment_ids = jnp.arange(local_segments, dtype=jnp.int32)
    same_brick = (targets[:, None] == targets[None, :]) & (
        segment_ids[None, :] < segment_ids[:, None]
    )
    rank_within = jnp.sum(same_brick.astype(jnp.int32), axis=1)
    places = targets * capacity + rank_within
    slot_total = brick_count * capacity
    slot_ids = jnp.arange(slot_total, dtype=jnp.int32)
    slot_hits = places[None, :] == slot_ids[:, None]
    packed_rows = jnp.sum(jnp.where(slot_hits, voxel_rows[None, :], 0), axis=1)
    contributions = spread_taps(values, kernels, kernel_taps).astype(jnp.bfloat16)
    hits = slot_hits.astype(jnp.bfloat16)
    packed = jnp.stack(
        [jnp.dot(hits, part, preferred_element_type=jnp.float32) for part in contributions], axis=1
    ).astype(jnp.bfloat16)
    exchange = lambda lines: lax.all_to_all(
        lines.reshape(brick_count, capacity, -1),
        ("img", "freq"),
        split_axis=0,
        concat_axis=0,
        tiled=True,
    )
    arrived_rows = exchange(packed_rows).reshape(-1)
    arrived = exchange(packed).reshape(slot_total, 2 * lane_count)
    row_member = arrived_rows[None, :] == jnp.arange(BROWS, dtype=jnp.int32)[:, None]
    volume = jnp.stack(
        [
            jnp.dot(
                row_member.astype(jnp.bfloat16),
                arrived[:, part * lane_count : (part + 1) * lane_count],
                preferred_element_type=jnp.float32,
            )
            for part in range(2)
        ]
    )
    return (own_rows, volume[None])


def solution(mesh):
    in_specs = (
        P(None, "img", "freq"),
        P(None, "img", "freq"),
        P("freq"),
        P("img"),
        P("freq", "img", None, None),
        P("freq", "img", None),
        P("freq", "img", None),
        P(),
    )
    out_specs = (P("freq", "img"), P(("img", "freq"), None, None, None))
    return jax.shard_map(
        on_device, mesh=mesh, in_specs=in_specs, out_specs=out_specs, check_vma=False
    )
```

```python
import jax
import jax.numpy as jnp
from jax import lax
from jax.experimental import pallas as pl
from jax.experimental.pallas import tpu as pltpu
from jax.sharding import PartitionSpec as P

MESH = pl.DeviceIdType.MESH
VMEM = pltpu.VMEM
DMA = pltpu.SemaphoreType.DMA
VMEM_BYTES = 60 * 1024 * 1024
RING = 4

BROWS = 2000
KEPT = 256
COARSE = 128
FINE = (64, 32, 16, 8)


tempering = 0.5
masked_logit = -1e30
contract_last = (((1,), (1,)), ((), ()))


def window_parts(prior_orient, orient_count):
    start = (prior_orient - orient_count // 8) % orient_count
    return start // COARSE, start % COARSE


def to_windows(scores, prior_orient):
    orient_count = scores.shape[0]
    coarse, fine = window_parts(prior_orient, orient_count)
    rows = KEPT + sum(FINE)
    ring = jnp.concatenate([scores, scores[: rows - COARSE]], axis=0)
    kept = ring[:rows]
    for block in range(1, orient_count // COARSE):
        kept = jnp.where((coarse == block)[None], ring[block * COARSE : block * COARSE + rows], kept)
    for step in FINE:
        rows -= step
        kept = jnp.where(((fine // step) % 2 == 1)[None], kept[step : step + rows], kept[:rows])
    return kept


def from_windows(kept, prior_orient, orient_count):
    coarse, fine = window_parts(prior_orient, orient_count)
    for step in FINE[::-1]:
        pad = jnp.zeros((step, kept.shape[1]), kept.dtype)
        kept = jnp.where(
            ((fine // step) % 2 == 1)[None],
            jnp.concatenate([pad, kept], axis=0),
            jnp.concatenate([kept, pad], axis=0),
        )
    kept = jnp.pad(kept, ((0, -kept.shape[0] % COARSE), (0, 0)))
    blocks = orient_count // COARSE
    parts = []
    for block in range(blocks):
        part = jnp.zeros((COARSE, kept.shape[1]), kept.dtype)
        for piece in range(kept.shape[0] // COARSE):
            part = jnp.where(
                (coarse == (block - piece) % blocks)[None],
                kept[piece * COARSE : (piece + 1) * COARSE],
                part,
            )
        parts.append(part)
    return jnp.concatenate(parts, axis=0)


def img_neighbours():
    me = lax.axis_index("img")
    z, x = me // RING, me % RING
    at = lambda other, shift: (z + other) % 2 * RING + (x + shift) % RING
    return at


def greet(axis, others):
    barrier = pltpu.get_barrier_semaphore()
    for other in others:
        pl.semaphore_signal(barrier, inc=1, device_id={axis: other}, device_id_type=MESH)
    pl.semaphore_wait(barrier, len(others))


def score_kernel(
    refs_ref, noise_ref, images_hbm, out_ref, images, gathered, weighted, energy,
    load_sem, own_sem, send_sem, recv_sem,
):
    at = img_neighbours()
    rows = refs_ref.shape[1]
    load = pltpu.make_async_copy(images_hbm, images, load_sem)
    load.start()
    own = pltpu.make_async_copy(refs_ref, gathered.at[at(0, 0)], own_sem)
    own.start()
    greet("img", [at(0, 1), at(0, 3), at(1, 0)])
    own.wait()

    def send(number, shard, part, target):
        copy = pltpu.make_async_remote_copy(
            src_ref=gathered.at[shard, part],
            dst_ref=gathered.at[shard, part],
            send_sem=send_sem.at[number],
            recv_sem=recv_sem.at[number],
            device_id={"img": target},
            device_id_type=MESH,
        )
        copy.start()
        return copy

    right, left, across = at(0, 1), at(0, 3), at(1, 0)
    mine = at(0, 0)
    own_right = [send(0, mine, 0, right), None]
    own_left = [None, send(1, mine, 1, left)]
    own_across = [send(2, mine, 0, across), None]
    own_right[1] = send(3, mine, 1, right)
    own_left[0] = send(4, mine, 0, left)
    own_across[1] = send(5, mine, 1, across)

    def weigh(shard, part, place, fresh):
        lines = 16

        def body(step, _):
            at_row = pl.multiple_of(step * lines, lines)
            value = gathered[shard, part, pl.ds(at_row, lines), :].astype(jnp.float32)
            scaled = value * noise_ref[...]
            weighted[pl.ds(pl.multiple_of(place * rows + at_row, lines), lines), :] = scaled.astype(
                jnp.bfloat16
            )
            total = jnp.sum(scaled * value, axis=1, keepdims=True)
            here = pl.ds(pl.multiple_of(place * rows + at_row, lines), lines)
            if fresh:
                energy[here, :] = jnp.broadcast_to(total, (lines, 128))
            else:
                energy[here, :] = energy[here, :] + total
            return 0

        lax.fori_loop(0, rows // lines, body, 0)

    def multiply(first, second, part, fresh):
        weigh(first, part, 0, fresh)
        weigh(second, part, 1, fresh)
        width = 256

        def body(step, _):
            column = pl.ds(pl.multiple_of(step * width, width), width)
            product = lax.dot_general(
                weighted[...], images[part, column, :], contract_last,
                preferred_element_type=jnp.float32,
            )
            if not fresh:
                product = product - 0.5 * jnp.tile(energy[...], (1, width // 128))
            for place, shard in enumerate((first, second)):
                block = product[place * rows : (place + 1) * rows]
                there = pl.ds(pl.multiple_of(shard * rows, 16), rows)
                if fresh:
                    out_ref[there, column] = block
                else:
                    out_ref[there, column] = out_ref[there, column] + block
            return 0

        lax.fori_loop(0, images.shape[1] // width, body, 0)

    own_right[0].wait_recv()
    next_right = send(6, at(0, 3), 0, right)
    own_left[1].wait_recv()
    next_left = send(7, at(0, 1), 1, left)
    load.wait()
    own_across[0].wait_recv()
    over_right = [send(8, at(1, 0), 0, right), None]
    over_left = [send(9, at(1, 0), 0, left), None]
    multiply(at(0, 0), at(1, 0), 0, True)
    own_across[1].wait_recv()
    over_right[1] = send(10, at(1, 0), 1, right)
    over_left[1] = send(11, at(1, 0), 1, left)
    multiply(at(0, 0), at(1, 0), 1, False)
    own_right[1].wait_recv()
    own_left[0].wait_recv()
    next_right.wait_recv()
    over_across = [send(12, at(0, 2), 0, across), None]
    next_left.wait_recv()
    over_across[1] = send(13, at(0, 2), 1, across)
    multiply(at(0, 1), at(0, 3), 0, True)
    multiply(at(0, 1), at(0, 3), 1, False)
    over_right[0].wait_recv()
    over_left[0].wait_recv()
    multiply(at(1, 1), at(1, 3), 0, True)
    over_right[1].wait_recv()
    over_left[1].wait_recv()
    multiply(at(1, 1), at(1, 3), 1, False)
    over_across[0].wait_recv()
    multiply(at(0, 2), at(1, 2), 0, True)
    over_across[1].wait_recv()
    multiply(at(0, 2), at(1, 2), 1, False)
    for copy in (
        own_right + own_left + own_across + [next_right, next_left]
        + over_right + over_left + over_across
    ):
        copy.wait_send()


def gathered_scores(references, noise_weight, images, image_groups):
    parts, rows, freqs = references.shape
    count = images.shape[1]
    return pl.pallas_call(
        score_kernel,
        out_shape=jax.ShapeDtypeStruct((image_groups * rows, count), jnp.float32),
        in_specs=[pl.BlockSpec(memory_space=VMEM)] * 2 + [pl.BlockSpec(memory_space=pl.ANY)],
        out_specs=pl.BlockSpec(memory_space=VMEM),
        scratch_shapes=[
            VMEM(images.shape, jnp.bfloat16),
            VMEM((image_groups, parts, rows, freqs), jnp.bfloat16),
            VMEM((2 * rows, freqs), jnp.bfloat16),
            VMEM((2 * rows, 128), jnp.float32),
            DMA(()),
            DMA(()),
            DMA((14,)),
            DMA((14,)),
        ],
        compiler_params=pltpu.CompilerParams(
            collective_id=0, has_side_effects=True, vmem_limit_bytes=VMEM_BYTES
        ),
    )(references, noise_weight.reshape(1, freqs), images)


def posterior_kernel(
    windows_ref, fine_ref, out_ref, pair_in, chip_out, chip_in,
    pair_send, pair_recv, chip_send, chip_recv, gat_send, gat_recv, sib_send, sib_recv,
):
    me = lax.axis_index("freq")
    core = me % 2
    z, y = me // 8, me // 2 % 4
    count = windows_ref.shape[0] // 16
    sibling = me + 1 - 2 * core
    spots = [(dz, dy) for dz, dy in ((1, 2), (1, 1), (1, 3), (0, 2), (1, 0), (0, 1), (0, 3), (0, 0))]
    target = lambda dz, dy: (z + dz) % 2 * 8 + (y + dy) % 4 * 2 + core
    source = lambda dz, dy: (z + dz) % 2 * 8 + (y + 4 - dy) % 4 * 2 + core
    greet("freq", [target(*spot) for spot in spots[:-1]] + [sibling])
    lines = lambda block: pl.ds(pl.multiple_of(block * count, 16), count)

    def send(src, dst, send_sem, recv_sem, other):
        copy = pltpu.make_async_remote_copy(
            src_ref=src, dst_ref=dst, send_sem=send_sem, recv_sem=recv_sem,
            device_id={"freq": other}, device_id_type=MESH,
        )
        copy.start()
        return copy

    pairs = []
    for n, spot in enumerate(spots):
        block = target(*spot) + 1 - 2 * core
        pairs.append(
            send(windows_ref.at[lines(block)], pair_in.at[n], pair_send.at[n], pair_recv.at[n], sibling)
        )
    chips = []
    for n, spot in enumerate(spots):
        pairs[n].wait_recv()
        total = windows_ref[lines(target(*spot)), :] + pair_in[n]
        if n == 7:
            break
        chip_out[n] = total
        chips.append(
            send(chip_out.at[n], chip_in.at[n], chip_send.at[n], chip_recv.at[n], target(*spot))
        )
    chip_out[7] = total
    scores = chip_out[7]
    for n in range(7):
        chips[6 - n].wait_recv()
        scores = scores + chip_in[6 - n]
    fine = fine_ref[...]
    position = lax.broadcasted_iota(jnp.int32, scores.shape, 1)
    inside = (position >= fine) & (position <= fine + 224)
    logits = jnp.where(inside, tempering * scores, masked_logit)
    raised = jnp.where(inside, jnp.exp(logits - jnp.max(logits, axis=1, keepdims=True)), 0.0)
    result = raised / jnp.sum(raised, axis=1, keepdims=True)
    out_ref[lines(me), :] = result.astype(jnp.bfloat16)
    gathers, relays = [], []
    for n, spot in enumerate(spots[:-1]):
        here = out_ref.at[lines(me)]
        gathers.append(send(here, here, gat_send.at[n], gat_recv.at[n], target(*spot)))
    here = out_ref.at[lines(me)]
    relays.append(send(here, here, sib_send.at[7], sib_recv.at[7], sibling))
    for n in range(6, -1, -1):
        gathers[n].wait_recv()
        here = out_ref.at[lines(source(*spots[n]))]
        relays.append(send(here, here, sib_send.at[n], sib_recv.at[n], sibling))
    for copy in relays:
        copy.wait_recv()
    for copy in pairs + chips + gathers + relays:
        copy.wait_send()


def windowed_posterior(windows, own_fine):
    rows, width = windows.shape
    count = rows // 16
    sems = [DMA((8,)) for _ in range(8)]
    return pl.pallas_call(
        posterior_kernel,
        out_shape=jax.ShapeDtypeStruct((rows, width), jnp.bfloat16),
        in_specs=[pl.BlockSpec(memory_space=VMEM)] * 2,
        out_specs=pl.BlockSpec(memory_space=VMEM),
        scratch_shapes=[VMEM((8, count, width), jnp.float32) for _ in range(3)] + sems,
        compiler_params=pltpu.CompilerParams(
            collective_id=1, has_side_effects=True, vmem_limit_bytes=VMEM_BYTES
        ),
    )(windows, own_fine)


def sums_kernel(
    rounded_ref, images_hbm, out_ref, images, lhs, part, first_in, side_in, half_in, near_in,
    last_in, load_sem, send_sem, recv_sem,
):
    at = img_neighbours()
    rows, freqs = out_ref.shape[1:]
    loads = []
    for n in range(2):
        loads.append(pltpu.make_async_copy(images_hbm.at[n], images.at[n], load_sem.at[n]))
        loads[-1].start()
    right, left, across = at(0, 1), at(0, 3), at(1, 0)
    greet("img", [right, left, across])

    def multiply(first, second, n):
        for place, (other, shift) in enumerate((first, second)):
            there = pl.ds(pl.multiple_of(at(other, shift) * rows, 16), rows)
            lhs[place * rows : (place + 1) * rows, :] = rounded_ref[there, :]
        width = 256

        def body(step, _):
            column = pl.ds(pl.multiple_of(step * width, width), width)
            product = jnp.dot(
                lhs[...], images[n, :, column], preferred_element_type=jnp.float32
            ).astype(jnp.bfloat16)
            for place, (other, shift) in enumerate((first, second)):
                part[other * 4 + shift, n, :, column] = product[place * rows : (place + 1) * rows]
            return 0

        lax.fori_loop(0, freqs // width, body, 0)

    copies = []

    def send(src, dst, target):
        number = len(copies)
        copy = pltpu.make_async_remote_copy(
            src_ref=src, dst_ref=dst, send_sem=send_sem.at[number], recv_sem=recv_sem.at[number],
            device_id={"img": target}, device_id_type=MESH,
        )
        copy.start()
        copies.append(copy)
        return copy

    def combine(dst, sources):
        lines = 16

        def body(step, _):
            here = pl.ds(pl.multiple_of(step * lines, lines), lines)
            total = sources[0][here, :].astype(jnp.float32)
            for source in sources[1:]:
                total = total + source[here, :].astype(jnp.float32)
            dst[here, :] = total.astype(dst.dtype)
            return 0

        lax.fori_loop(0, rows // lines, body, 0)

    first, sides, near = [], [[], []], [[None, None], [None, None]]
    for n in range(2):
        loads[n].wait()
        multiply((1, 2), (0, 2), n)
        first.append(send(part.at[6, n], first_in.at[n], across))
    for n in range(2):
        multiply((1, 1), (1, 3), n)
        sides[0].append(send(part.at[5, n], side_in.at[0, n], right))
        sides[1].append(send(part.at[7, n], side_in.at[1, n], left))
    for n in range(2):
        multiply((0, 1), (0, 3), n)
    halves = []
    first[0].wait_recv()
    combine(part.at[2, 0], [part.at[2, 0], first_in.at[0]])
    halves.append(send(part.at[2, 0], half_in.at[0], left))
    for n in range(2):
        multiply((1, 0), (0, 0), n)
    first[1].wait_recv()
    combine(part.at[2, 1], [part.at[2, 1], first_in.at[1]])
    halves.append(send(part.at[2, 1], half_in.at[1], right))
    near[0][0] = send(part.at[1, 0], near_in.at[0, 0], right)
    near[1][1] = send(part.at[3, 1], near_in.at[1, 1], left)
    last = []
    for n in range(2):
        sides[0][n].wait_recv()
        sides[1][n].wait_recv()
        combine(part.at[4, n], [part.at[4, n], side_in.at[0, n], side_in.at[1, n]])
        last.append(send(part.at[4, n], last_in.at[n], across))
    halves[0].wait_recv()
    combine(part.at[3, 0], [part.at[3, 0], half_in.at[0]])
    near[1][0] = send(part.at[3, 0], near_in.at[1, 0], left)
    halves[1].wait_recv()
    combine(part.at[1, 1], [part.at[1, 1], half_in.at[1]])
    near[0][1] = send(part.at[1, 1], near_in.at[0, 1], right)
    for n in range(2):
        near[0][n].wait_recv()
        near[1][n].wait_recv()
        last[n].wait_recv()
        combine(
            out_ref.at[n], [part.at[0, n], near_in.at[0, n], near_in.at[1, n], last_in.at[n]]
        )
    for copy in copies:
        copy.wait_send()


def scattered_sums(rounded, images, image_groups):
    rows = rounded.shape[0] // image_groups
    parts, count, freqs = images.shape
    block = (parts, rows, freqs)
    return pl.pallas_call(
        sums_kernel,
        out_shape=jax.ShapeDtypeStruct(block, jnp.float32),
        in_specs=[pl.BlockSpec(memory_space=VMEM), pl.BlockSpec(memory_space=pl.ANY)],
        out_specs=pl.BlockSpec(memory_space=VMEM),
        scratch_shapes=[
            VMEM(images.shape, jnp.bfloat16),
            VMEM((2 * rows, count), jnp.bfloat16),
            VMEM((image_groups, *block), jnp.bfloat16),
            VMEM(block, jnp.bfloat16),
            VMEM((2, *block), jnp.bfloat16),
            VMEM(block, jnp.bfloat16),
            VMEM((2, *block), jnp.bfloat16),
            VMEM(block, jnp.bfloat16),
            DMA((2,)),
            DMA((14,)),
            DMA((14,)),
        ],
        compiler_params=pltpu.CompilerParams(
            collective_id=2, has_side_effects=True, vmem_limit_bytes=VMEM_BYTES
        ),
    )(rounded, images)


def exchange_kernel(
    sums_ref, factor_ref, place_ref, table_ref, out_ref, values, packed, arrived, lines_in,
    members, terms, total, send_sem, recv_sem, line_send, line_recv, own_sem,
):
    groups, wide = 8, 16
    img, freq = lax.axis_index("img"), lax.axis_index("freq")
    slots = packed.shape[1] // 2
    segments = values.shape[0]
    rows, lanes = sums_ref.shape[1], sums_ref.shape[2] // (segments // sums_ref.shape[1])
    barrier = pltpu.get_barrier_semaphore()

    def everyone(visit):
        def outer(di, _):
            def inner(df, _):
                @pl.when((di > 0) | (df > 0))
                def _():
                    visit(di, (img + di) % groups, (freq + df) % wide)

                return 0

            return lax.fori_loop(0, wide, inner, 0)

        lax.fori_loop(0, groups, outer, 0)

    everyone(
        lambda di, to_img, to_freq: pl.semaphore_signal(
            barrier, inc=1, device_id={"img": to_img, "freq": to_freq}, device_id_type=MESH
        )
    )
    lane = lax.broadcasted_iota(jnp.int32, (rows, lanes), 1)
    for q in range(segments // rows):
        for part in range(2):
            value = sums_ref[part, :, q * lanes : (q + 1) * lanes]
            shifted = [
                jnp.where(lane < lanes - 1, pltpu.roll(value, lanes - 1, 1), 0.0),
                value,
                jnp.where(lane >= 1, pltpu.roll(value, 1, 1), 0.0),
                jnp.where(lane >= 2, pltpu.roll(value, 2, 1), 0.0),
            ]
            result = factor_ref[q, :, 0:1] * shifted[0]
            for tap in range(1, 4):
                result = result + factor_ref[q, :, tap : tap + 1] * shifted[tap]
            values[q * rows : (q + 1) * rows, part * lanes : (part + 1) * lanes] = result.astype(
                jnp.bfloat16
            )
    me = img * wide + freq
    pl.semaphore_wait(barrier, groups * wide - 1)

    def send_line(di, to_img, to_freq):
        pltpu.make_async_remote_copy(
            src_ref=table_ref.at[to_img * wide + to_freq],
            dst_ref=lines_in.at[me],
            send_sem=line_send,
            recv_sem=line_recv,
            device_id={"img": to_img, "freq": to_freq},
            device_id_type=MESH,
        ).start()

    everyone(send_line)
    lines_in[me] = table_ref[me]

    def send_group(di, _):
        to_img = (img + di) % groups
        some = wide // 2

        def pack(half, _):
            base = (to_img * wide + half * some) * slots
            slot = base + lax.broadcasted_iota(jnp.int32, (some * slots, 1), 0)
            found = jnp.zeros((some * slots, 2 * lanes), jnp.float32)
            step = 256
            for first in range(0, segments, step):
                hit = jnp.where(place_ref[:, first : first + step] == slot, 1.0, 0.0)
                found = found + jnp.dot(
                    hit.astype(jnp.bfloat16), values[first : first + step, :],
                    preferred_element_type=jnp.float32,
                )
            for brick in range(some):
                block = found[brick * slots : (brick + 1) * slots]
                packed[to_img * wide + half * some + brick] = jnp.concatenate(
                    [block[:, :lanes], block[:, lanes:]], axis=0
                ).astype(jnp.bfloat16)
            return 0

        lax.fori_loop(0, 2, pack, 0)

        def inner(df, _):
            to_freq = (freq + df) % wide

            @pl.when((di > 0) | (df > 0))
            def _():
                pltpu.make_async_remote_copy(
                    src_ref=packed.at[to_img * wide + to_freq],
                    dst_ref=arrived.at[me],
                    send_sem=send_sem,
                    recv_sem=recv_sem.at[di],
                    device_id={"img": to_img, "freq": to_freq},
                    device_id_type=MESH,
                ).start()

            return 0

        return lax.fori_loop(0, wide, inner, 0)

    lax.fori_loop(0, groups, send_group, 0)
    own = pltpu.make_async_copy(packed.at[me], arrived.at[me], own_sem)
    own.start()
    most = pl.ds(0, groups * wide - 1)
    pltpu.make_async_copy(lines_in.at[most], lines_in.at[most], line_recv).wait()
    pltpu.make_async_copy(table_ref.at[most], table_ref.at[most], line_send).wait()
    place = lax.broadcasted_iota(jnp.int32, (1, 128), 1)
    chunks = wide * slots // 128
    row_step = 400

    def make_members(group, _):
        row_lines = [jnp.zeros((1, 128), jnp.int32) for _ in range(chunks)]
        for member in range(wide):
            line = lines_in[group * wide + member]
            chunk, first = member * slots // 128, member * slots % 128
            turned = pltpu.roll(line, first, 1) if first else line
            row_lines[chunk] = jnp.where(
                (place >= first) & (place < first + slots), turned, row_lines[chunk]
            )
            if first + slots > 128:
                row_lines[chunk + 1] = jnp.where(
                    place < first + slots - 128, turned, row_lines[chunk + 1]
                )
        row_lines = jnp.concatenate(row_lines, axis=1)

        def fill(step, _):
            first = pl.multiple_of(step * 16, 16)
            voxel = first + lax.broadcasted_iota(jnp.int32, (16, 1), 0)
            members[group, pl.ds(first, 16), :] = jnp.where(row_lines == voxel, 1.0, 0.0).astype(
                jnp.bfloat16
            )
            return 0

        return lax.fori_loop(0, BROWS // 16, fill, 0)

    lax.fori_loop(0, groups, make_members, 0)
    for di in range(groups):
        group = (img + groups - di) % groups
        count = wide - 1 if di == 0 else wide
        some = pl.ds(0, count)
        pltpu.make_async_copy(arrived.at[some], arrived.at[some], recv_sem.at[di]).wait()
        if di == 0:
            own.wait()
        for pair in range(wide // 2):
            blocks = [
                arrived[group * wide + 2 * pair + n].astype(jnp.float32) for n in range(2)
            ]
            for part in range(2):
                both = [block[part * slots : (part + 1) * slots] for block in blocks]
                terms[2 * pair * slots : 2 * (pair + 1) * slots, part * lanes : (part + 1) * lanes] = (
                    jnp.concatenate(both, axis=0).astype(jnp.bfloat16)
                )

        def add(step, _):
            here = pl.ds(pl.multiple_of(step * row_step, 16), row_step)
            found = jnp.dot(members[group, here, :], terms[...], preferred_element_type=jnp.float32)
            if di > 0:
                found = found + total[here, :]
            if di < groups - 1:
                total[here, :] = found
            else:
                out_ref[0, 0, here, :] = found[:, :lanes]
                out_ref[0, 1, here, :] = found[:, lanes:]
            return 0

        lax.fori_loop(0, BROWS // row_step, add, 0)
    pltpu.make_async_copy(packed.at[most], packed.at[most], send_sem).wait()


def exchanged_volume(sums, factors, places, table, slots):
    bricks = table.shape[0]
    segments = places.shape[1]
    lanes = 128
    return pl.pallas_call(
        exchange_kernel,
        out_shape=jax.ShapeDtypeStruct((1, 2, BROWS, lanes), jnp.float32),
        in_specs=[pl.BlockSpec(memory_space=VMEM)] * 4,
        out_specs=pl.BlockSpec(memory_space=VMEM),
        scratch_shapes=[
            VMEM((segments, 2 * lanes), jnp.bfloat16),
            VMEM((bricks, 2 * slots, lanes), jnp.bfloat16),
            VMEM((bricks, 2 * slots, lanes), jnp.bfloat16),
            VMEM((bricks, 1, 128), jnp.int32),
            VMEM((8, BROWS, 16 * slots), jnp.bfloat16),
            VMEM((16 * slots, 2 * lanes), jnp.bfloat16),
            VMEM((BROWS, 2 * lanes), jnp.float32),
            DMA(()),
            DMA((8,)),
            DMA(()),
            DMA(()),
            DMA(()),
        ],
        compiler_params=pltpu.CompilerParams(
            collective_id=3, has_side_effects=True, vmem_limit_bytes=VMEM_BYTES
        ),
    )(sums, factors, places, table)


def tap_factors(kernels, kernel_taps):
    member = kernels[..., None] == jnp.arange(kernel_taps.shape[0], dtype=jnp.int32)
    return jnp.sum(jnp.where(member[..., None], kernel_taps, 0.0), axis=-2)


def on_device(
    images,
    references,
    noise_weight,
    prior_orient,
    segment_brick,
    segment_row,
    segment_kernel,
    kernel_taps,
):
    image_groups = lax.axis_size("img")
    freq_groups = lax.axis_size("freq")
    local_orients = references.shape[1]
    orient_count = local_orients * image_groups
    share_rows = orient_count // freq_groups
    share_images = images.shape[1] // freq_groups
    partial_scores = gathered_scores(references, noise_weight, images, image_groups)
    windows = to_windows(partial_scores, prior_orient).T
    own_prior = lax.dynamic_slice_in_dim(
        prior_orient, lax.axis_index("freq") * share_images, share_images, 0
    )
    own_fine = window_parts(own_prior, orient_count)[1] % FINE[-1]
    kept = windowed_posterior(windows, own_fine[:, None]).T
    rounded = from_windows(kept, prior_orient, orient_count)
    own_rows = lax.dynamic_slice_in_dim(
        rounded, lax.axis_index("freq") * share_rows, share_rows, 0
    ).astype(jnp.float32)
    weighted_sums = scattered_sums(rounded, images, image_groups)
    segment_blocks = segment_row.shape[2]
    by_block = lambda per_segment: per_segment.reshape(local_orients, segment_blocks).T
    local_segments = local_orients * segment_blocks
    targets = by_block(segment_brick).reshape(-1)
    voxel_rows = by_block(segment_row).reshape(-1)
    factors = tap_factors(by_block(segment_kernel), kernel_taps)
    brick_count = image_groups * freq_groups
    capacity = max(2, 5 * local_segments // (2 * brick_count))
    slots = -(-capacity // 8) * 8
    segment_ids = jnp.arange(local_segments, dtype=jnp.int32)
    same_brick = (targets[:, None] == targets[None, :]) & (
        segment_ids[None, :] < segment_ids[:, None]
    )
    places = targets * slots + jnp.sum(same_brick.astype(jnp.int32), axis=1)
    slot_ids = jnp.arange(brick_count * slots, dtype=jnp.int32)
    hits = places[None, :] == slot_ids[:, None]
    table = jnp.sum(jnp.where(hits, voxel_rows[None, :], 0), axis=1).reshape(brick_count, 1, slots)
    table = jnp.pad(table, ((0, 0), (0, 0), (0, 128 - slots)))
    volume = exchanged_volume(weighted_sums, factors, places[None, :], table, slots)
    return (own_rows, volume)


def solution(mesh):
    in_specs = (
        P(None, "img", "freq"),
        P(None, "img", "freq"),
        P("freq"),
        P("img"),
        P("freq", "img", None, None),
        P("freq", "img", None),
        P("freq", "img", None),
        P(),
    )
    out_specs = (P("freq", "img"), P(("img", "freq"), None, None, None))
    return jax.shard_map(
        on_device, mesh=mesh, in_specs=in_specs, out_specs=out_specs, check_vma=False
    )
```

```python
import jax
import jax.numpy as jnp
from jax import lax
from jax.experimental import pallas as pl
from jax.experimental.pallas import tpu as pltpu
from jax.sharding import PartitionSpec as P

MESH = pl.DeviceIdType.MESH
VMEM = pltpu.VMEM
DMA = pltpu.SemaphoreType.DMA
VMEM_BYTES = 60 * 1024 * 1024
RING = 4

BROWS = 2000
KEPT = 256
SLOTS = 40
MOVED = 32
ROW_SHIFT = 3
BRICK_SHIFT = 14
COARSE = 128
FINE = (64, 32, 16, 8)


tempering = 0.5
masked_logit = -1e30
contract_last = (((1,), (1,)), ((), ()))


def window_parts(prior_orient, orient_count):
    start = (prior_orient - orient_count // 8) % orient_count
    return start // COARSE, start % COARSE


def img_neighbours():
    me = lax.axis_index("img")
    z, x = me // RING, me % RING
    at = lambda other, shift: (z + other) % 2 * RING + (x + shift) % RING
    return at


def greet(others):
    barrier = pltpu.get_barrier_semaphore()
    for axis, other in others:
        pl.semaphore_signal(barrier, inc=1, device_id={axis: other}, device_id_type=MESH)
    pl.semaphore_wait(barrier, len(others))


def slot_tables(code_row, code_column, place_ref, lines, table_ref):
    segments = code_column.shape[0]
    bricks, step = table_ref.shape[0], 64
    named = jnp.right_shift(code_row[:, :segments], BRICK_SHIFT)
    ahead = lax.broadcasted_iota(jnp.int32, (1, segments), 1)

    def count_before(turn, rank):
        here = pl.ds(pl.multiple_of(turn * step, step), step)
        index = turn * step + lax.broadcasted_iota(jnp.int32, (step, 1), 0)
        same = (jnp.right_shift(code_column[here, :], BRICK_SHIFT) == named) & (index < ahead)
        return rank + jnp.sum(jnp.where(same, 1, 0), axis=0, keepdims=True)

    rank = lax.fori_loop(
        0, segments // step, count_before, jnp.zeros((1, segments), jnp.int32)
    )
    place_ref[...] = named * SLOTS + rank
    voxel = jnp.right_shift(code_row[:, :segments] & ((1 << BRICK_SHIFT) - 1), ROW_SHIFT)
    high = jnp.right_shift(voxel, 4)
    low = voxel - high * 16
    line = lax.broadcasted_iota(jnp.int32, (bricks, 1), 0)
    of_rank = jnp.where(rank == line, 1.0, 0.0).astype(jnp.bfloat16)
    table = jnp.zeros((bricks, 128), jnp.float32)
    for scale, digits in ((16.0, high), (1.0, low)):
        of_brick = jnp.where(named == line, digits.astype(jnp.float32), 0.0).astype(jnp.bfloat16)
        table = table + scale * lax.dot_general(
            of_brick, of_rank, contract_last, preferred_element_type=jnp.float32
        )
    lines[...] = table.astype(jnp.int32)

    def copy_line(brick, _):
        table_ref[brick] = lines[pl.ds(brick, 1), :]
        return 0

    lax.fori_loop(0, bricks, copy_line, 0)


def to_windows(scores_ref, prior_ref, windows_ref):
    orient_count = scores_ref.shape[0]

    def body(step, _):
        column = pl.ds(pl.multiple_of(step * 128, 128), 128)
        coarse, fine = window_parts(prior_ref[:, column], orient_count)
        rows = KEPT + sum(FINE)
        kept = scores_ref[:rows, column]
        for block in range(1, orient_count // COARSE):
            first = block * COARSE
            piece = scores_ref[first : min(first + rows, orient_count), column]
            if first + rows > orient_count:
                wrapped = scores_ref[: first + rows - orient_count, column]
                piece = jnp.concatenate([piece, wrapped], axis=0)
            kept = jnp.where(coarse == block, piece, kept)
        for size in FINE:
            rows -= size
            kept = jnp.where(fine // size % 2 == 1, kept[size : size + rows], kept[:rows])
        position = lax.broadcasted_iota(jnp.int32, (KEPT, 1), 0) - fine % FINE[-1]
        inside = (position >= 0) & (position <= 2 * (orient_count // 8))
        windows_ref[column, :] = jnp.where(inside, kept, masked_logit).T
        return 0

    lax.fori_loop(0, scores_ref.shape[1] // 128, body, 0)


def from_windows(kept_ref, prior_ref, wide_ref, rounded_ref):
    orient_count = wide_ref.shape[0]

    def body(step, _):
        column = pl.ds(pl.multiple_of(step * 128, 128), 128)
        coarse, fine = window_parts(prior_ref[:, column], orient_count)
        kept = kept_ref[column, :].astype(jnp.float32).T
        for size in FINE[::-1]:
            pad = jnp.zeros((size, 128), jnp.float32)
            kept = jnp.where(
                fine // size % 2 == 1,
                jnp.concatenate([pad, kept], axis=0),
                jnp.concatenate([kept, pad], axis=0),
            )
        kept = jnp.concatenate([kept, jnp.zeros((-kept.shape[0] % COARSE, 128), jnp.float32)], axis=0)
        blocks = orient_count // COARSE
        for block in range(blocks):
            part = jnp.zeros((COARSE, 128), jnp.float32)
            for piece in range(kept.shape[0] // COARSE):
                part = jnp.where(
                    coarse == (block - piece) % blocks,
                    kept[piece * COARSE : (piece + 1) * COARSE],
                    part,
                )
            here = slice(block * COARSE, (block + 1) * COARSE)
            wide_ref[here, column] = part
            rounded_ref[here, column] = part.astype(jnp.bfloat16)
        return 0

    lax.fori_loop(0, wide_ref.shape[1] // 128, body, 0)


def posterior_kernel(
    refs_ref, noise_ref, code_row, code_column, images_hbm,
    rounded_ref, rows_ref, place_ref, table_ref,
    images, gathered, weighted, energy, out_ref, windows_ref, kept_ref, lines,
    pair_in, chip_out, chip_in, load_sem, own_sem, send_sem, recv_sem,
    pair_send, pair_recv, chip_send, chip_recv, gat_send, gat_recv, sib_send, sib_recv,
):
    freq = lax.axis_index("freq")
    core = freq % 2
    z, y = freq // 8, freq // 2 % 4
    count = windows_ref.shape[0] // 16
    sibling = freq + 1 - 2 * core
    spots = [(dz, dy) for dz, dy in ((1, 2), (1, 1), (1, 3), (0, 2), (1, 0), (0, 1), (0, 3), (0, 0))]
    target = lambda dz, dy: (z + dz) % 2 * 8 + (y + dy) % 4 * 2 + core
    source = lambda dz, dy: (z + dz) % 2 * 8 + (y + 4 - dy) % 4 * 2 + core
    at = img_neighbours()
    rows = refs_ref.shape[1]
    load = pltpu.make_async_copy(images_hbm, images, load_sem)
    load.start()
    own = pltpu.make_async_copy(refs_ref, gathered.at[at(0, 0)], own_sem)
    own.start()
    greet(
        [("img", at(0, 1)), ("img", at(0, 3)), ("img", at(1, 0)), ("freq", sibling)]
        + [("freq", target(*spot)) for spot in spots[:-1]]
    )
    own.wait()

    def forward(number, shard, part, target, first=0, last=rows):
        some = gathered.at[shard, part, pl.ds(first, last - first)]
        copy = pltpu.make_async_remote_copy(
            src_ref=some,
            dst_ref=some,
            send_sem=send_sem.at[number],
            recv_sem=recv_sem.at[number],
            device_id={"img": target},
            device_id_type=MESH,
        )
        copy.start()
        return copy

    right, left, across = at(0, 1), at(0, 3), at(1, 0)
    mine = at(0, 0)
    own_right = [forward(0, mine, 0, right), None]
    own_left = [None, forward(1, mine, 1, left)]
    own_across = [forward(2, mine, 0, across), None]
    own_right[1] = forward(3, mine, 1, right)
    own_left[0] = forward(4, mine, 0, left)
    own_across[1] = forward(5, mine, 1, across)

    def weigh(shard, part, place, fresh, bank):
        lines = 16
        for first in range(0, rows, lines):
            value = gathered[shard, part, first : first + lines, :].astype(jnp.float32)
            scaled = value * noise_ref[...]
            here = slice(place * rows + first, place * rows + first + lines)
            weighted[here, :] = scaled.astype(jnp.bfloat16)
            squares = scaled * value
            total = squares[:, :128]
            for lane in range(128, squares.shape[1], 128):
                total = total + squares[:, lane : lane + 128]
            energy[bank, here, :] = total if fresh else energy[bank, here, :] + total

    def multiply(first, second, part, fresh, bank=0):
        weigh(first, part, 0, fresh, bank)
        weigh(second, part, 1, fresh, bank)
        if not fresh:
            half = 0.5 * jnp.sum(energy[bank], axis=1, keepdims=True)
        width = 256

        def body(step, _):
            column = pl.ds(pl.multiple_of(step * width, width), width)
            product = lax.dot_general(
                weighted[...], images[part, column, :], contract_last,
                preferred_element_type=jnp.float32,
            )
            if not fresh:
                product = product - half
            for place, shard in enumerate((first, second)):
                block = product[place * rows : (place + 1) * rows]
                there = pl.ds(pl.multiple_of(shard * rows, 16), rows)
                if fresh:
                    out_ref[there, column] = block
                else:
                    out_ref[there, column] = out_ref[there, column] + block
            return 0

        lax.fori_loop(0, images.shape[1] // width, body, 0)

    slot_tables(code_row, code_column, place_ref, lines, table_ref)
    own_right[0].wait_recv()
    next_right = forward(6, at(0, 3), 0, right)
    own_left[1].wait_recv()
    next_left = forward(7, at(0, 1), 1, left)
    extra = [forward(14, at(0, 1), 1, across, rows - MOVED), None]
    load.wait()
    own_across[0].wait_recv()
    over_right = [forward(8, at(1, 0), 0, right), None]
    over_left = [forward(9, at(1, 0), 0, left), None]
    multiply(at(0, 0), at(1, 0), 0, True)
    own_across[1].wait_recv()
    over_right[1] = forward(10, at(1, 0), 1, right, 0, rows - MOVED)
    over_left[1] = forward(11, at(1, 0), 1, left, 0, rows - MOVED)
    own_right[1].wait_recv()
    extra[1] = forward(15, at(0, 3), 1, across, rows - MOVED)
    multiply(at(0, 0), at(1, 0), 1, False)
    own_left[0].wait_recv()
    multiply(at(0, 1), at(0, 3), 0, True)
    multiply(at(0, 1), at(0, 3), 1, False)
    next_right.wait_recv()
    over_across = [forward(12, at(0, 2), 0, across), None]
    next_left.wait_recv()
    over_across[1] = forward(13, at(0, 2), 1, across)
    over_right[0].wait_recv()
    over_left[0].wait_recv()
    multiply(at(1, 1), at(1, 3), 0, True)
    over_across[0].wait_recv()
    multiply(at(0, 2), at(1, 2), 0, True, 1)
    for copy in (over_right[1], over_left[1], extra[0], extra[1]):
        copy.wait_recv()
    multiply(at(1, 1), at(1, 3), 1, False)
    over_across[1].wait_recv()
    multiply(at(0, 2), at(1, 2), 1, False, 1)
    for copy in (
        own_right + own_left + own_across + [next_right, next_left]
        + over_right + over_left + over_across + extra
    ):
        copy.wait_send()
    prior_ref = code_row.at[:, pl.ds(code_column.shape[0], out_ref.shape[1])]
    to_windows(out_ref, prior_ref, windows_ref)
    block_lines = lambda block: pl.ds(pl.multiple_of(block * count, 16), count)

    def send(src, dst, send_sem, recv_sem, other):
        copy = pltpu.make_async_remote_copy(
            src_ref=src, dst_ref=dst, send_sem=send_sem, recv_sem=recv_sem,
            device_id={"freq": other}, device_id_type=MESH,
        )
        copy.start()
        return copy

    pairs = []
    for n, spot in enumerate(spots):
        block = target(*spot) + 1 - 2 * core
        pairs.append(
            send(windows_ref.at[block_lines(block)], pair_in.at[n], pair_send.at[n], pair_recv.at[n], sibling)
        )
    chips = []
    for n, spot in enumerate(spots):
        pairs[n].wait_recv()
        total = windows_ref[block_lines(target(*spot)), :] + pair_in[n]
        if n == 7:
            break
        chip_out[n] = total
        chips.append(
            send(chip_out.at[n], chip_in.at[n], chip_send.at[n], chip_recv.at[n], target(*spot))
        )
    chip_out[7] = total
    scores = chip_out[7]
    for n in range(7):
        chips[6 - n].wait_recv()
        scores = scores + chip_in[6 - n]
    inside = scores > 0.5 * masked_logit
    logits = jnp.where(inside, tempering * scores, masked_logit)
    raised = jnp.where(inside, jnp.exp(logits - jnp.max(logits, axis=1, keepdims=True)), 0.0)
    result = raised / jnp.sum(raised, axis=1, keepdims=True)
    kept_ref[block_lines(freq), :] = result.astype(jnp.bfloat16)
    gathers, relays = [], []
    for n, spot in enumerate(spots[:-1]):
        here = kept_ref.at[block_lines(freq)]
        gathers.append(send(here, here, gat_send.at[n], gat_recv.at[n], target(*spot)))
    here = kept_ref.at[block_lines(freq)]
    relays.append(send(here, here, sib_send.at[7], sib_recv.at[7], sibling))
    for n in range(6, -1, -1):
        gathers[n].wait_recv()
        here = kept_ref.at[block_lines(source(*spots[n]))]
        relays.append(send(here, here, sib_send.at[n], sib_recv.at[n], sibling))
    for copy in relays:
        copy.wait_recv()
    for copy in pairs + chips + gathers + relays:
        copy.wait_send()
    from_windows(kept_ref, prior_ref, out_ref, rounded_ref)
    share = rows_ref.shape[0]
    rows_ref[...] = out_ref[pl.ds(pl.multiple_of(freq * share, 8), share), :]


def posteriors(
    references, noise_weight, code_row, code_column, images, image_groups, freq_groups
):
    parts, rows, freqs = references.shape
    count = images.shape[1]
    orients, segments = image_groups * rows, code_column.shape[0]
    bricks = image_groups * freq_groups
    share = count // freq_groups
    return pl.pallas_call(
        posterior_kernel,
        out_shape=(
            jax.ShapeDtypeStruct((orients, count), jnp.bfloat16),
            jax.ShapeDtypeStruct((orients * share // count, count), jnp.float32),
            jax.ShapeDtypeStruct((1, segments), jnp.int32),
            jax.ShapeDtypeStruct((bricks, 1, 128), jnp.int32),
        ),
        in_specs=[pl.BlockSpec(memory_space=VMEM)] * 4 + [pl.BlockSpec(memory_space=pl.ANY)],
        out_specs=[pl.BlockSpec(memory_space=VMEM)] * 4,
        scratch_shapes=[
            VMEM(images.shape, jnp.bfloat16),
            VMEM((image_groups, parts, rows, freqs), jnp.bfloat16),
            VMEM((2 * rows, freqs), jnp.bfloat16),
            VMEM((2, 2 * rows, 128), jnp.float32),
            VMEM((orients, count), jnp.float32),
            VMEM((count, KEPT), jnp.float32),
            VMEM((count, KEPT), jnp.bfloat16),
            VMEM((bricks, 128), jnp.int32),
        ]
        + [VMEM((8, share, KEPT), jnp.float32) for _ in range(3)]
        + [DMA(()), DMA(()), DMA((16,)), DMA((16,))]
        + [DMA((8,)) for _ in range(8)],
        compiler_params=pltpu.CompilerParams(
            collective_id=0, has_side_effects=True, vmem_limit_bytes=VMEM_BYTES
        ),
    )(references, noise_weight.reshape(1, freqs), code_row, code_column, images)


def volume_kernel(
    rounded_ref, code_column, taps_ref, place_ref, table_ref, images_hbm, out_ref,
    images, lhs, part, first_in, side_in, half_in, near_in, last_in, extra_in, sums_ref,
    values, packed, arrived, lines_in, members, terms, factor_ref,
    load_sem, group_send, group_recv, send_sem, recv_sem, line_send, line_recv, own_sem,
):
    groups, wide = 8, 16
    img, freq = lax.axis_index("img"), lax.axis_index("freq")
    barrier = pltpu.get_barrier_semaphore()
    at = img_neighbours()
    rows, freqs = sums_ref.shape[1:]
    loads = []
    for n in range(2):
        loads.append(pltpu.make_async_copy(images_hbm.at[n], images.at[n], load_sem.at[n]))
        loads[-1].start()
    right, left, across = at(0, 1), at(0, 3), at(1, 0)

    def everyone(visit):
        def outer(di, _):
            def inner(df, _):
                @pl.when((di > 0) | (df > 0))
                def _():
                    visit(di, (img + di) % groups, (freq + df) % wide)

                return 0

            return lax.fori_loop(0, wide, inner, 0)

        lax.fori_loop(0, groups, outer, 0)

    everyone(
        lambda di, to_img, to_freq: pl.semaphore_signal(
            barrier, inc=1, device_id={"img": to_img, "freq": to_freq}, device_id_type=MESH
        )
    )

    def multiply(first, second, n):
        for place, (other, shift) in enumerate((first, second)):
            there = pl.ds(pl.multiple_of(at(other, shift) * rows, 16), rows)
            lhs[place * rows : (place + 1) * rows, :] = rounded_ref[there, :]
        width = 256

        def body(step, _):
            column = pl.ds(pl.multiple_of(step * width, width), width)
            product = jnp.dot(
                lhs[...], images[n, :, column], preferred_element_type=jnp.float32
            ).astype(jnp.bfloat16)
            for place, (other, shift) in enumerate((first, second)):
                part[other * 4 + shift, n, :, column] = product[place * rows : (place + 1) * rows]
            return 0

        lax.fori_loop(0, freqs // width, body, 0)

    copies = []

    def send(src, dst, target):
        number = len(copies)
        copy = pltpu.make_async_remote_copy(
            src_ref=src, dst_ref=dst, send_sem=group_send.at[number], recv_sem=group_recv.at[number],
            device_id={"img": target}, device_id_type=MESH,
        )
        copy.start()
        copies.append(copy)
        return copy

    def combine(dst, sources, count=rows):
        lines = 16

        def body(step, _):
            here = pl.ds(pl.multiple_of(step * lines, lines), lines)
            total = sources[0][here, :].astype(jnp.float32)
            for source in sources[1:]:
                total = total + source[here, :].astype(jnp.float32)
            dst[here, :] = total.astype(dst.dtype)
            return 0

        lax.fori_loop(0, count // lines, body, 0)

    stay = rows - MOVED
    kept, moved = pl.ds(0, stay), pl.ds(stay, MOVED)
    first, sides, near, extra = [], [[], []], [[None, None], [None, None]], []
    for n in range(2):
        loads[n].wait()
        multiply((1, 1), (1, 3), n)
        if n == 0:
            pl.semaphore_wait(barrier, groups * wide - 1)
        some = pl.ds(0, rows) if n == 0 else kept
        for way, (here, there) in enumerate(((5, right), (7, left))):
            sides[way].append(send(part.at[here, n, some], side_in.at[way, n, some], there))
        multiply((1, 2), (0, 2), n)
        first.append(send(part.at[6, n], first_in.at[n], across))
    for way, here in enumerate((5, 7)):
        extra.append(send(part.at[here, 1, moved], extra_in.at[way], across))
    me = img * wide + freq

    def send_line(di, to_img, to_freq):
        pltpu.make_async_remote_copy(
            src_ref=table_ref.at[to_img * wide + to_freq],
            dst_ref=lines_in.at[me],
            send_sem=line_send,
            recv_sem=line_recv,
            device_id={"img": to_img, "freq": to_freq},
            device_id_type=MESH,
        ).start()

    everyone(send_line)
    lines_in[me] = table_ref[me]

    for n in range(2):
        multiply((0, 1), (0, 3), n)
    halves = []
    first[0].wait_recv()
    combine(part.at[2, 0], [part.at[2, 0], first_in.at[0]])
    halves.append(send(part.at[2, 0], half_in.at[0], left))
    for n in range(2):
        multiply((1, 0), (0, 0), n)
    first[1].wait_recv()
    combine(part.at[2, 1], [part.at[2, 1], first_in.at[1]])
    halves.append(send(part.at[2, 1], half_in.at[1], right))
    near[0][0] = send(part.at[1, 0], near_in.at[0, 0], right)
    for way, here in enumerate((1, 3)):
        extra[way].wait_recv()
        some = part.at[here, 1, moved]
        combine(some, [some, extra_in.at[way]], MOVED)
    near[1][1] = send(part.at[3, 1], near_in.at[1, 1], left)
    phases, tap_count = taps_ref.shape
    for q in range(factor_ref.shape[0]):
        kernel = code_column[q * rows : (q + 1) * rows, :] & ((1 << ROW_SHIFT) - 1)
        for tap in range(tap_count):
            factor = jnp.zeros((rows, 1), jnp.float32)
            for phase in range(phases):
                factor = jnp.where(kernel == phase, taps_ref[phase, tap], factor)
            factor_ref[q, :, tap : tap + 1] = factor
    last = []
    for n in range(2):
        sides[0][n].wait_recv()
        sides[1][n].wait_recv()
        combine(
            part.at[4, n], [part.at[4, n], side_in.at[0, n], side_in.at[1, n]],
            rows if n == 0 else stay,
        )
        last.append(send(part.at[4, n], last_in.at[n], across))
    halves[0].wait_recv()
    combine(part.at[3, 0], [part.at[3, 0], half_in.at[0]])
    near[1][0] = send(part.at[3, 0], near_in.at[1, 0], left)
    halves[1].wait_recv()
    combine(part.at[1, 1], [part.at[1, 1], half_in.at[1]])
    near[0][1] = send(part.at[1, 1], near_in.at[0, 1], right)
    for n in range(2):
        near[0][n].wait_recv()
        near[1][n].wait_recv()
        last[n].wait_recv()
        combine(
            sums_ref.at[n], [part.at[0, n], near_in.at[0, n], near_in.at[1, n], last_in.at[n]]
        )
    for copy in copies:
        copy.wait_send()
    slots = packed.shape[1] // 2
    segments = values.shape[0]
    lanes = freqs // (segments // rows)
    lane = lax.broadcasted_iota(jnp.int32, (rows, lanes), 1)
    for q in range(segments // rows):
        for part in range(2):
            value = sums_ref[part, :, q * lanes : (q + 1) * lanes]
            shifted = [
                jnp.where(lane < lanes - 1, pltpu.roll(value, lanes - 1, 1), 0.0),
                value,
                jnp.where(lane >= 1, pltpu.roll(value, 1, 1), 0.0),
                jnp.where(lane >= 2, pltpu.roll(value, 2, 1), 0.0),
            ]
            result = factor_ref[q, :, 0:1] * shifted[0]
            for tap in range(1, 4):
                result = result + factor_ref[q, :, tap : tap + 1] * shifted[tap]
            values[q * rows : (q + 1) * rows, part * lanes : (part + 1) * lanes] = result.astype(
                jnp.bfloat16
            )
    def send_group(di, _):
        to_img = (img + di) % groups
        some = wide // 2

        def pack(half, _):
            base = (to_img * wide + half * some) * slots
            slot = base + lax.broadcasted_iota(jnp.int32, (some * slots, 1), 0)
            found = jnp.zeros((some * slots, 2 * lanes), jnp.float32)
            step = 256
            for first in range(0, segments, step):
                hit = jnp.where(place_ref[:, first : first + step] == slot, 1.0, 0.0)
                found = found + jnp.dot(
                    hit.astype(jnp.bfloat16), values[first : first + step, :],
                    preferred_element_type=jnp.float32,
                )
            for brick in range(some):
                block = found[brick * slots : (brick + 1) * slots]
                packed[to_img * wide + half * some + brick] = jnp.concatenate(
                    [block[:, :lanes], block[:, lanes:]], axis=0
                ).astype(jnp.bfloat16)
            return 0

        lax.fori_loop(0, 2, pack, 0)

        def inner(df, _):
            to_freq = (freq + df) % wide

            @pl.when((di > 0) | (df > 0))
            def _():
                pltpu.make_async_remote_copy(
                    src_ref=packed.at[to_img * wide + to_freq],
                    dst_ref=arrived.at[me],
                    send_sem=send_sem,
                    recv_sem=recv_sem.at[di],
                    device_id={"img": to_img, "freq": to_freq},
                    device_id_type=MESH,
                ).start()

            return 0

        return lax.fori_loop(0, wide, inner, 0)

    lax.fori_loop(0, groups, send_group, 0)
    own = pltpu.make_async_copy(packed.at[me], arrived.at[me], own_sem)
    own.start()
    most = pl.ds(0, groups * wide - 1)
    pltpu.make_async_copy(lines_in.at[most], lines_in.at[most], line_recv).wait()
    pltpu.make_async_copy(table_ref.at[most], table_ref.at[most], line_send).wait()
    place = lax.broadcasted_iota(jnp.int32, (1, 128), 1)
    chunks = wide * slots // 128
    row_step = 400
    held = members.shape[0]

    def make_members(di, _):
        group = (img + groups - di) % groups
        row_lines = [jnp.zeros((1, 128), jnp.int32) for _ in range(chunks)]
        for member in range(wide):
            line = lines_in[group * wide + member]
            chunk, first = member * slots // 128, member * slots % 128
            turned = pltpu.roll(line, first, 1) if first else line
            row_lines[chunk] = jnp.where(
                (place >= first) & (place < first + slots), turned, row_lines[chunk]
            )
            if first + slots > 128:
                row_lines[chunk + 1] = jnp.where(
                    place < first + slots - 128, turned, row_lines[chunk + 1]
                )
        row_lines = jnp.concatenate(row_lines, axis=1)

        def fill(step, _):
            first = pl.multiple_of(step * 16, 16)
            voxel = first + lax.broadcasted_iota(jnp.int32, (16, 1), 0)
            members[di % held, pl.ds(first, 16), :] = jnp.where(row_lines == voxel, 1.0, 0.0).astype(
                jnp.bfloat16
            )
            return 0

        return lax.fori_loop(0, BROWS // 16, fill, 0)

    lax.fori_loop(0, held, make_members, 0)
    for di in range(groups):
        group = (img + groups - di) % groups
        count = wide - 1 if di == 0 else wide
        some = pl.ds(0, count)
        pltpu.make_async_copy(arrived.at[some], arrived.at[some], recv_sem.at[di]).wait()
        if di == 0:
            own.wait()
        for pair in range(wide // 2):
            blocks = [
                arrived[group * wide + 2 * pair + n].astype(jnp.float32) for n in range(2)
            ]
            for part in range(2):
                both = [block[part * slots : (part + 1) * slots] for block in blocks]
                terms[2 * pair * slots : 2 * (pair + 1) * slots, part * lanes : (part + 1) * lanes] = (
                    jnp.concatenate(both, axis=0).astype(jnp.bfloat16)
                )

        def add(step, _):
            here = pl.ds(pl.multiple_of(step * row_step, 16), row_step)
            found = jnp.dot(members[di % held, here, :], terms[...], preferred_element_type=jnp.float32)
            if di > 0:
                found = found + jnp.concatenate([out_ref[0, 0, here, :], out_ref[0, 1, here, :]], axis=1)
            out_ref[0, 0, here, :] = found[:, :lanes]
            out_ref[0, 1, here, :] = found[:, lanes:]
            return 0

        lax.fori_loop(0, BROWS // row_step, add, 0)
        if di + held < groups:
            make_members(di + held, 0)
    pltpu.make_async_copy(packed.at[most], packed.at[most], send_sem).wait()


def back_projected(rounded, images, code_column, kernel_taps, places, table, image_groups):
    rows = rounded.shape[0] // image_groups
    parts, count, freqs = images.shape
    block = (parts, rows, freqs)
    bricks, segments, lanes = table.shape[0], places.shape[1], 128
    return pl.pallas_call(
        volume_kernel,
        out_shape=jax.ShapeDtypeStruct((1, parts, BROWS, lanes), jnp.float32),
        in_specs=[pl.BlockSpec(memory_space=VMEM)] * 2
        + [pl.BlockSpec(memory_space=pltpu.SMEM)]
        + [pl.BlockSpec(memory_space=VMEM)] * 2
        + [pl.BlockSpec(memory_space=pl.ANY)],
        out_specs=pl.BlockSpec(memory_space=VMEM),
        scratch_shapes=[
            VMEM(images.shape, jnp.bfloat16),
            VMEM((2 * rows, count), jnp.bfloat16),
            VMEM((image_groups, *block), jnp.bfloat16),
            VMEM(block, jnp.bfloat16),
            VMEM((2, *block), jnp.bfloat16),
            VMEM(block, jnp.bfloat16),
            VMEM((2, *block), jnp.bfloat16),
            VMEM(block, jnp.bfloat16),
            VMEM((2, MOVED, freqs), jnp.bfloat16),
            VMEM(block, jnp.float32),
            VMEM((segments, 2 * lanes), jnp.bfloat16),
            VMEM((bricks, 2 * SLOTS, lanes), jnp.bfloat16),
            VMEM((bricks, 2 * SLOTS, lanes), jnp.bfloat16),
            VMEM((bricks, 1, 128), jnp.int32),
            VMEM((4, BROWS, 16 * SLOTS), jnp.bfloat16),
            VMEM((16 * SLOTS, 2 * lanes), jnp.bfloat16),
            VMEM((segments // rows, rows, kernel_taps.shape[1]), jnp.float32),
            DMA((2,)),
            DMA((16,)),
            DMA((16,)),
            DMA(()),
            DMA((8,)),
            DMA(()),
            DMA(()),
            DMA(()),
        ],
        compiler_params=pltpu.CompilerParams(
            collective_id=2, has_side_effects=True, vmem_limit_bytes=VMEM_BYTES
        ),
    )(rounded, code_column, kernel_taps, places, table, images)


def on_device(
    images,
    references,
    noise_weight,
    prior_orient,
    segment_brick,
    segment_row,
    segment_kernel,
    kernel_taps,
):
    image_groups = lax.axis_size("img")
    freq_groups = lax.axis_size("freq")
    local_orients = references.shape[1]
    segment_blocks = segment_row.shape[2]
    codes = (segment_brick[..., 0] << BRICK_SHIFT) + (segment_row << ROW_SHIFT) + segment_kernel
    codes = codes.reshape(local_orients, segment_blocks).T.reshape(-1)
    code_row = jnp.concatenate([codes, prior_orient])[None, :]
    code_column = codes[:, None]
    rounded, own_rows, places, table = posteriors(
        references, noise_weight, code_row, code_column, images, image_groups, freq_groups
    )
    volume = back_projected(
        rounded, images, code_column, kernel_taps, places, table, image_groups
    )
    return (own_rows, volume)


def solution(mesh):
    in_specs = (
        P(None, "img", "freq"),
        P(None, "img", "freq"),
        P("freq"),
        P("img"),
        P("freq", "img", None, None),
        P("freq", "img", None),
        P("freq", "img", None),
        P(),
    )
    out_specs = (P("freq", "img"), P(("img", "freq"), None, None, None))
    return jax.shard_map(
        on_device, mesh=mesh, in_specs=in_specs, out_specs=out_specs, check_vma=False
    )
```

```python
import jax
import jax.numpy as jnp
from jax import lax
from jax.experimental import pallas as pl
from jax.experimental.pallas import tpu as pltpu
from jax.sharding import PartitionSpec as P

MESH = pl.DeviceIdType.MESH
VMEM = pltpu.VMEM
DMA = pltpu.SemaphoreType.DMA
VMEM_BYTES = 60 * 1024 * 1024
RING = 4

BROWS = 2000
KEPT = 256
SLOTS = 40
MOVED = 32
ROW_SHIFT = 3
BRICK_SHIFT = 14
COARSE = 128
FINE = (64, 32, 16, 8)


tempering = 0.5
masked_logit = -1e30
contract_last = (((1,), (1,)), ((), ()))


def window_parts(prior_orient, orient_count):
    start = (prior_orient - orient_count // 8) % orient_count
    return start // COARSE, start % COARSE


def img_neighbours():
    me = lax.axis_index("img")
    z, x = me // RING, me % RING
    at = lambda other, shift: (z + other) % 2 * RING + (x + shift) % RING
    return at


def greet(others):
    barrier = pltpu.get_barrier_semaphore()
    for axis, other in others:
        pl.semaphore_signal(barrier, inc=1, device_id={axis: other}, device_id_type=MESH)
    pl.semaphore_wait(barrier, len(others))


def slot_tables(code_row, code_column, place_ref, lines, table_ref):
    segments = code_column.shape[0]
    bricks, step = table_ref.shape[0], 64
    named = jnp.right_shift(code_row[:, :segments], BRICK_SHIFT)
    ahead = lax.broadcasted_iota(jnp.int32, (1, segments), 1)

    def count_before(turn, rank):
        here = pl.ds(pl.multiple_of(turn * step, step), step)
        index = turn * step + lax.broadcasted_iota(jnp.int32, (step, 1), 0)
        same = (jnp.right_shift(code_column[here, :], BRICK_SHIFT) == named) & (index < ahead)
        return rank + jnp.sum(jnp.where(same, 1, 0), axis=0, keepdims=True)

    rank = lax.fori_loop(
        0, segments // step, count_before, jnp.zeros((1, segments), jnp.int32)
    )
    place_ref[...] = named * SLOTS + rank
    voxel = jnp.right_shift(code_row[:, :segments] & ((1 << BRICK_SHIFT) - 1), ROW_SHIFT)
    high = jnp.right_shift(voxel, 4)
    low = voxel - high * 16
    line = lax.broadcasted_iota(jnp.int32, (bricks, 1), 0)
    of_rank = jnp.where(rank == line, 1.0, 0.0).astype(jnp.bfloat16)
    table = jnp.zeros((bricks, 128), jnp.float32)
    for scale, digits in ((16.0, high), (1.0, low)):
        of_brick = jnp.where(named == line, digits.astype(jnp.float32), 0.0).astype(jnp.bfloat16)
        table = table + scale * lax.dot_general(
            of_brick, of_rank, contract_last, preferred_element_type=jnp.float32
        )
    lines[...] = table.astype(jnp.int32)

    def copy_line(brick, _):
        table_ref[brick] = lines[pl.ds(brick, 1), :]
        return 0

    lax.fori_loop(0, bricks, copy_line, 0)


def to_windows(scores_ref, prior_ref, windows_ref):
    orient_count = scores_ref.shape[0]

    def body(step, _):
        column = pl.ds(pl.multiple_of(step * 128, 128), 128)
        coarse, fine = window_parts(prior_ref[:, column], orient_count)
        rows = KEPT + sum(FINE)
        kept = scores_ref[:rows, column]
        for block in range(1, orient_count // COARSE):
            first = block * COARSE
            piece = scores_ref[first : min(first + rows, orient_count), column]
            if first + rows > orient_count:
                wrapped = scores_ref[: first + rows - orient_count, column]
                piece = jnp.concatenate([piece, wrapped], axis=0)
            kept = jnp.where(coarse == block, piece, kept)
        for size in FINE:
            rows -= size
            kept = jnp.where(fine // size % 2 == 1, kept[size : size + rows], kept[:rows])
        position = lax.broadcasted_iota(jnp.int32, (KEPT, 1), 0) - fine % FINE[-1]
        inside = (position >= 0) & (position <= 2 * (orient_count // 8))
        windows_ref[column, :] = jnp.where(inside, kept, masked_logit).T
        return 0

    lax.fori_loop(0, scores_ref.shape[1] // 128, body, 0)


def from_windows(kept_ref, prior_ref, wide_ref, rounded_ref):
    orient_count = wide_ref.shape[0]

    def body(step, _):
        column = pl.ds(pl.multiple_of(step * 128, 128), 128)
        coarse, fine = window_parts(prior_ref[:, column], orient_count)
        kept = kept_ref[column, :].astype(jnp.float32).T
        for size in FINE[::-1]:
            pad = jnp.zeros((size, 128), jnp.float32)
            kept = jnp.where(
                fine // size % 2 == 1,
                jnp.concatenate([pad, kept], axis=0),
                jnp.concatenate([kept, pad], axis=0),
            )
        kept = jnp.concatenate([kept, jnp.zeros((-kept.shape[0] % COARSE, 128), jnp.float32)], axis=0)
        blocks = orient_count // COARSE
        for block in range(blocks):
            part = jnp.zeros((COARSE, 128), jnp.float32)
            for piece in range(kept.shape[0] // COARSE):
                part = jnp.where(
                    coarse == (block - piece) % blocks,
                    kept[piece * COARSE : (piece + 1) * COARSE],
                    part,
                )
            here = slice(block * COARSE, (block + 1) * COARSE)
            wide_ref[here, column] = part
            rounded_ref[here, column] = part.astype(jnp.bfloat16)
        return 0

    lax.fori_loop(0, wide_ref.shape[1] // 128, body, 0)


def posterior_kernel(
    refs_ref, noise_ref, code_row, code_column, images_hbm,
    rounded_ref, rows_ref, place_ref, table_ref,
    images, gathered, weighted, energy, out_ref, windows_ref, kept_ref, lines,
    pair_in, chip_out, chip_in, load_sem, own_sem, send_sem, recv_sem,
    pair_send, pair_recv, chip_send, chip_recv, gat_send, gat_recv, sib_send, sib_recv,
):
    freq = lax.axis_index("freq")
    core = freq % 2
    z, y = freq // 8, freq // 2 % 4
    count = windows_ref.shape[0] // 16
    sibling = freq + 1 - 2 * core
    spots = [(dz, dy) for dz, dy in ((1, 2), (1, 1), (1, 3), (0, 2), (1, 0), (0, 1), (0, 3), (0, 0))]
    target = lambda dz, dy: (z + dz) % 2 * 8 + (y + dy) % 4 * 2 + core
    source = lambda dz, dy: (z + dz) % 2 * 8 + (y + 4 - dy) % 4 * 2 + core
    at = img_neighbours()
    rows = refs_ref.shape[1]
    load = pltpu.make_async_copy(images_hbm, images, load_sem)
    load.start()
    own = pltpu.make_async_copy(refs_ref, gathered.at[at(0, 0)], own_sem)
    own.start()
    greet(
        [("img", at(0, 1)), ("img", at(0, 3)), ("img", at(1, 0)), ("freq", sibling)]
        + [("freq", target(*spot)) for spot in spots[:-1]]
    )
    own.wait()

    def forward(number, shard, part, target, first=0, last=rows):
        some = gathered.at[shard, part, pl.ds(first, last - first)]
        copy = pltpu.make_async_remote_copy(
            src_ref=some,
            dst_ref=some,
            send_sem=send_sem.at[number],
            recv_sem=recv_sem.at[number],
            device_id={"img": target},
            device_id_type=MESH,
        )
        copy.start()
        return copy

    right, left, across = at(0, 1), at(0, 3), at(1, 0)
    mine = at(0, 0)
    own_right = [forward(0, mine, 0, right), None]
    own_left = [None, forward(1, mine, 1, left)]
    own_across = [forward(2, mine, 0, across), None]
    own_right[1] = forward(3, mine, 1, right)
    own_left[0] = forward(4, mine, 0, left)
    own_across[1] = forward(5, mine, 1, across)

    def weigh(shard, part, place, fresh, bank):
        lines = 16
        for first in range(0, rows, lines):
            value = gathered[shard, part, first : first + lines, :].astype(jnp.float32)
            scaled = value * noise_ref[...]
            here = slice(place * rows + first, place * rows + first + lines)
            weighted[here, :] = scaled.astype(jnp.bfloat16)
            squares = scaled * value
            total = squares[:, :128]
            for lane in range(128, squares.shape[1], 128):
                total = total + squares[:, lane : lane + 128]
            energy[bank, here, :] = total if fresh else energy[bank, here, :] + total

    def multiply(first, second, part, fresh, bank=0):
        weigh(first, part, 0, fresh, bank)
        weigh(second, part, 1, fresh, bank)
        if not fresh:
            half = 0.5 * jnp.sum(energy[bank], axis=1, keepdims=True)
        width = 256

        def body(step, _):
            column = pl.ds(pl.multiple_of(step * width, width), width)
            product = lax.dot_general(
                weighted[...], images[part, column, :], contract_last,
                preferred_element_type=jnp.float32,
            )
            if not fresh:
                product = product - half
            for place, shard in enumerate((first, second)):
                block = product[place * rows : (place + 1) * rows]
                there = pl.ds(pl.multiple_of(shard * rows, 16), rows)
                if fresh:
                    out_ref[there, column] = block
                else:
                    out_ref[there, column] = out_ref[there, column] + block
            return 0

        lax.fori_loop(0, images.shape[1] // width, body, 0)

    slot_tables(code_row, code_column, place_ref, lines, table_ref)
    own_right[0].wait_recv()
    next_right = forward(6, at(0, 3), 0, right)
    own_left[1].wait_recv()
    next_left = forward(7, at(0, 1), 1, left)
    extra = [forward(14, at(0, 1), 1, across, rows - MOVED), None]
    load.wait()
    own_across[0].wait_recv()
    over_right = [forward(8, at(1, 0), 0, right), None]
    over_left = [forward(9, at(1, 0), 0, left), None]
    multiply(at(0, 0), at(1, 0), 0, True)
    own_across[1].wait_recv()
    over_right[1] = forward(10, at(1, 0), 1, right, 0, rows - MOVED)
    over_left[1] = forward(11, at(1, 0), 1, left, 0, rows - MOVED)
    own_right[1].wait_recv()
    extra[1] = forward(15, at(0, 3), 1, across, rows - MOVED)
    multiply(at(0, 0), at(1, 0), 1, False)
    own_left[0].wait_recv()
    multiply(at(0, 1), at(0, 3), 0, True)
    multiply(at(0, 1), at(0, 3), 1, False)
    next_right.wait_recv()
    over_across = [forward(12, at(0, 2), 0, across), None]
    next_left.wait_recv()
    over_across[1] = forward(13, at(0, 2), 1, across)
    over_right[0].wait_recv()
    over_left[0].wait_recv()
    multiply(at(1, 1), at(1, 3), 0, True)
    over_across[0].wait_recv()
    multiply(at(0, 2), at(1, 2), 0, True, 1)
    for copy in (over_right[1], over_left[1], extra[0], extra[1]):
        copy.wait_recv()
    multiply(at(1, 1), at(1, 3), 1, False)
    over_across[1].wait_recv()
    multiply(at(0, 2), at(1, 2), 1, False, 1)
    for copy in (
        own_right + own_left + own_across + [next_right, next_left]
        + over_right + over_left + over_across + extra
    ):
        copy.wait_send()
    prior_ref = code_row.at[:, pl.ds(code_column.shape[0], out_ref.shape[1])]
    to_windows(out_ref, prior_ref, windows_ref)
    block_lines = lambda block: pl.ds(pl.multiple_of(block * count, 16), count)

    def send(src, dst, send_sem, recv_sem, other):
        copy = pltpu.make_async_remote_copy(
            src_ref=src, dst_ref=dst, send_sem=send_sem, recv_sem=recv_sem,
            device_id={"freq": other}, device_id_type=MESH,
        )
        copy.start()
        return copy

    pairs = []
    for n, spot in enumerate(spots):
        block = target(*spot) + 1 - 2 * core
        pairs.append(
            send(windows_ref.at[block_lines(block)], pair_in.at[n], pair_send.at[n], pair_recv.at[n], sibling)
        )
    chips = []
    for n, spot in enumerate(spots):
        pairs[n].wait_recv()
        total = windows_ref[block_lines(target(*spot)), :] + pair_in[n]
        if n == 7:
            break
        chip_out[n] = total
        chips.append(
            send(chip_out.at[n], chip_in.at[n], chip_send.at[n], chip_recv.at[n], target(*spot))
        )
    chip_out[7] = total
    scores = chip_out[7]
    for n in range(7):
        chips[6 - n].wait_recv()
        scores = scores + chip_in[6 - n]
    inside = scores > 0.5 * masked_logit
    logits = jnp.where(inside, tempering * scores, masked_logit)
    raised = jnp.where(inside, jnp.exp(logits - jnp.max(logits, axis=1, keepdims=True)), 0.0)
    result = raised / jnp.sum(raised, axis=1, keepdims=True)
    kept_ref[block_lines(freq), :] = result.astype(jnp.bfloat16)
    gathers, relays = [], []
    for n, spot in enumerate(spots[:-1]):
        here = kept_ref.at[block_lines(freq)]
        gathers.append(send(here, here, gat_send.at[n], gat_recv.at[n], target(*spot)))
    here = kept_ref.at[block_lines(freq)]
    relays.append(send(here, here, sib_send.at[7], sib_recv.at[7], sibling))
    for n in range(6, -1, -1):
        gathers[n].wait_recv()
        here = kept_ref.at[block_lines(source(*spots[n]))]
        relays.append(send(here, here, sib_send.at[n], sib_recv.at[n], sibling))
    for copy in relays:
        copy.wait_recv()
    for copy in pairs + chips + gathers + relays:
        copy.wait_send()
    from_windows(kept_ref, prior_ref, out_ref, rounded_ref)
    share = rows_ref.shape[0]
    rows_ref[...] = out_ref[pl.ds(pl.multiple_of(freq * share, 8), share), :]


def posteriors(
    references, noise_weight, code_row, code_column, images, image_groups, freq_groups
):
    parts, rows, freqs = references.shape
    count = images.shape[1]
    orients, segments = image_groups * rows, code_column.shape[0]
    bricks = image_groups * freq_groups
    share = count // freq_groups
    return pl.pallas_call(
        posterior_kernel,
        out_shape=(
            jax.ShapeDtypeStruct((orients, count), jnp.bfloat16),
            jax.ShapeDtypeStruct((orients * share // count, count), jnp.float32),
            jax.ShapeDtypeStruct((1, segments), jnp.int32),
            jax.ShapeDtypeStruct((bricks, 1, 128), jnp.int32),
        ),
        in_specs=[pl.BlockSpec(memory_space=VMEM)] * 4 + [pl.BlockSpec(memory_space=pl.ANY)],
        out_specs=[pl.BlockSpec(memory_space=VMEM)] * 4,
        scratch_shapes=[
            VMEM(images.shape, jnp.bfloat16),
            VMEM((image_groups, parts, rows, freqs), jnp.bfloat16),
            VMEM((2 * rows, freqs), jnp.bfloat16),
            VMEM((2, 2 * rows, 128), jnp.float32),
            VMEM((orients, count), jnp.float32),
            VMEM((count, KEPT), jnp.float32),
            VMEM((count, KEPT), jnp.bfloat16),
            VMEM((bricks, 128), jnp.int32),
        ]
        + [VMEM((8, share, KEPT), jnp.float32) for _ in range(3)]
        + [DMA(()), DMA(()), DMA((16,)), DMA((16,))]
        + [DMA((8,)) for _ in range(8)],
        compiler_params=pltpu.CompilerParams(
            collective_id=0, has_side_effects=True, vmem_limit_bytes=VMEM_BYTES
        ),
    )(references, noise_weight.reshape(1, freqs), code_row, code_column, images)


def volume_kernel(
    rounded_ref, code_column, taps_ref, place_ref, table_ref, images_hbm, out_ref,
    images, lhs, part, first_in, side_in, half_in, near_in, last_in, extra_in, sums_ref,
    values, packed, arrived, lines_in, members, terms, factor_ref,
    load_sem, group_send, group_recv, send_sem, recv_sem, line_send, line_recv, own_sem,
):
    groups, wide = 8, 16
    img, freq = lax.axis_index("img"), lax.axis_index("freq")
    barrier = pltpu.get_barrier_semaphore()
    at = img_neighbours()
    rows, freqs = sums_ref.shape[1:]
    loads = []
    for n in range(2):
        loads.append(pltpu.make_async_copy(images_hbm.at[n], images.at[n], load_sem.at[n]))
        loads[-1].start()
    right, left, across = at(0, 1), at(0, 3), at(1, 0)

    def everyone(visit):
        def outer(di, _):
            def inner(df, _):
                @pl.when((di > 0) | (df > 0))
                def _():
                    visit(di, (img + di) % groups, (freq + df) % wide)

                return 0

            return lax.fori_loop(0, wide, inner, 0)

        lax.fori_loop(0, groups, outer, 0)

    everyone(
        lambda di, to_img, to_freq: pl.semaphore_signal(
            barrier, inc=1, device_id={"img": to_img, "freq": to_freq}, device_id_type=MESH
        )
    )

    def multiply(first, second, n):
        for place, (other, shift) in enumerate((first, second)):
            there = pl.ds(pl.multiple_of(at(other, shift) * rows, 16), rows)
            lhs[place * rows : (place + 1) * rows, :] = rounded_ref[there, :]
        width = 256

        def body(step, _):
            column = pl.ds(pl.multiple_of(step * width, width), width)
            product = jnp.dot(
                lhs[...], images[n, :, column], preferred_element_type=jnp.float32
            ).astype(jnp.bfloat16)
            for place, (other, shift) in enumerate((first, second)):
                part[other * 4 + shift, n, :, column] = product[place * rows : (place + 1) * rows]
            return 0

        lax.fori_loop(0, freqs // width, body, 0)

    copies = []

    def send(src, dst, target):
        number = len(copies)
        copy = pltpu.make_async_remote_copy(
            src_ref=src, dst_ref=dst, send_sem=group_send.at[number], recv_sem=group_recv.at[number],
            device_id={"img": target}, device_id_type=MESH,
        )
        copy.start()
        copies.append(copy)
        return copy

    def combine(dst, sources, count=rows):
        lines = 16

        def body(step, _):
            here = pl.ds(pl.multiple_of(step * lines, lines), lines)
            total = sources[0][here, :].astype(jnp.float32)
            for source in sources[1:]:
                total = total + source[here, :].astype(jnp.float32)
            dst[here, :] = total.astype(dst.dtype)
            return 0

        lax.fori_loop(0, count // lines, body, 0)

    stay = rows - MOVED
    kept, moved = pl.ds(0, stay), pl.ds(stay, MOVED)
    first, sides, near, extra = [], [[], []], [[None, None], [None, None]], []
    for n in range(2):
        loads[n].wait()
        multiply((1, 1), (1, 3), n)
        if n == 0:
            pl.semaphore_wait(barrier, groups * wide - 1)
        some = pl.ds(0, rows) if n == 0 else kept
        for way, (here, there) in enumerate(((5, right), (7, left))):
            sides[way].append(send(part.at[here, n, some], side_in.at[way, n, some], there))
        multiply((1, 2), (0, 2), n)
        first.append(send(part.at[6, n], first_in.at[n], across))
    for way, here in enumerate((5, 7)):
        extra.append(send(part.at[here, 1, moved], extra_in.at[way], across))
    me = img * wide + freq

    def send_line(di, to_img, to_freq):
        pltpu.make_async_remote_copy(
            src_ref=table_ref.at[to_img * wide + to_freq],
            dst_ref=lines_in.at[me],
            send_sem=line_send,
            recv_sem=line_recv,
            device_id={"img": to_img, "freq": to_freq},
            device_id_type=MESH,
        ).start()

    everyone(send_line)
    lines_in[me] = table_ref[me]

    for n in range(2):
        multiply((0, 1), (0, 3), n)
    halves = []
    first[0].wait_recv()
    combine(part.at[2, 0], [part.at[2, 0], first_in.at[0]])
    halves.append(send(part.at[2, 0], half_in.at[0], left))
    for n in range(2):
        multiply((1, 0), (0, 0), n)
    first[1].wait_recv()
    combine(part.at[2, 1], [part.at[2, 1], first_in.at[1]])
    halves.append(send(part.at[2, 1], half_in.at[1], right))
    near[0][0] = send(part.at[1, 0], near_in.at[0, 0], right)
    for way, here in enumerate((1, 3)):
        extra[way].wait_recv()
        some = part.at[here, 1, moved]
        combine(some, [some, extra_in.at[way]], MOVED)
    near[1][1] = send(part.at[3, 1], near_in.at[1, 1], left)
    phases, tap_count = taps_ref.shape
    for q in range(factor_ref.shape[0]):
        kernel = code_column[q * rows : (q + 1) * rows, :] & ((1 << ROW_SHIFT) - 1)
        for tap in range(tap_count):
            factor = jnp.zeros((rows, 1), jnp.float32)
            for phase in range(phases):
                factor = jnp.where(kernel == phase, taps_ref[phase, tap], factor)
            factor_ref[q, :, tap : tap + 1] = factor
    last = []
    for n in range(2):
        sides[0][n].wait_recv()
        sides[1][n].wait_recv()
        combine(
            part.at[4, n], [part.at[4, n], side_in.at[0, n], side_in.at[1, n]],
            rows if n == 0 else stay,
        )
        last.append(send(part.at[4, n], last_in.at[n], across))
    slots = packed.shape[1] // 2
    order = (0, 1, 2, 3, 4, 5, 6, 7)
    most = pl.ds(0, groups * wide - 1)
    place = lax.broadcasted_iota(jnp.int32, (1, 128), 1)
    chunks = wide * slots // 128
    row_step = 1008
    held = members.shape[0]

    def make_members(turn):
        group = (img + groups - order[turn]) % groups
        row_lines = [jnp.zeros((1, 128), jnp.int32) for _ in range(chunks)]
        for member in range(wide):
            line = lines_in[group * wide + member]
            chunk, first = member * slots // 128, member * slots % 128
            turned = pltpu.roll(line, first, 1) if first else line
            row_lines[chunk] = jnp.where(
                (place >= first) & (place < first + slots), turned, row_lines[chunk]
            )
            if first + slots > 128:
                row_lines[chunk + 1] = jnp.where(
                    place < first + slots - 128, turned, row_lines[chunk + 1]
                )
        row_lines = jnp.concatenate(row_lines, axis=1)

        def fill(step, _):
            first = pl.multiple_of(step * 16, 16)
            voxel = first + lax.broadcasted_iota(jnp.int32, (16, 1), 0)
            members[turn % held, pl.ds(first, 16), :] = jnp.where(row_lines == voxel, 1.0, 0.0).astype(
                jnp.bfloat16
            )
            return 0

        lax.fori_loop(0, BROWS // 16, fill, 0)

    pltpu.make_async_copy(lines_in.at[most], lines_in.at[most], line_recv).wait()
    pltpu.make_async_copy(table_ref.at[most], table_ref.at[most], line_send).wait()
    for turn in range(held):
        make_members(turn)
    halves[0].wait_recv()
    combine(part.at[3, 0], [part.at[3, 0], half_in.at[0]])
    near[1][0] = send(part.at[3, 0], near_in.at[1, 0], left)
    halves[1].wait_recv()
    combine(part.at[1, 1], [part.at[1, 1], half_in.at[1]])
    near[0][1] = send(part.at[1, 1], near_in.at[0, 1], right)
    for n in range(2):
        near[0][n].wait_recv()
        near[1][n].wait_recv()
        last[n].wait_recv()
        combine(
            sums_ref.at[n], [part.at[0, n], near_in.at[0, n], near_in.at[1, n], last_in.at[n]]
        )
    for copy in copies:
        copy.wait_send()
    segments = values.shape[0]
    lanes = freqs // (segments // rows)
    lane = lax.broadcasted_iota(jnp.int32, (rows, lanes), 1)
    for q in range(segments // rows):
        for part in range(2):
            value = sums_ref[part, :, q * lanes : (q + 1) * lanes]
            shifted = [
                jnp.where(lane < lanes - 1, pltpu.roll(value, lanes - 1, 1), 0.0),
                value,
                jnp.where(lane >= 1, pltpu.roll(value, 1, 1), 0.0),
                jnp.where(lane >= 2, pltpu.roll(value, 2, 1), 0.0),
            ]
            result = factor_ref[q, :, 0:1] * shifted[0]
            for tap in range(1, 4):
                result = result + factor_ref[q, :, tap : tap + 1] * shifted[tap]
            values[q * rows : (q + 1) * rows, part * lanes : (part + 1) * lanes] = result.astype(
                jnp.bfloat16
            )
    def send_group(di):
        to_img = (img + di) % groups
        some = wide // 2

        def pack(half, _):
            base = (to_img * wide + half * some) * slots
            slot = base + lax.broadcasted_iota(jnp.int32, (some * slots, 1), 0)
            found = jnp.zeros((some * slots, 2 * lanes), jnp.float32)
            step = 256
            for first in range(0, segments, step):
                hit = jnp.where(place_ref[:, first : first + step] == slot, 1.0, 0.0)
                found = found + jnp.dot(
                    hit.astype(jnp.bfloat16), values[first : first + step, :],
                    preferred_element_type=jnp.float32,
                )
            for brick in range(some):
                block = found[brick * slots : (brick + 1) * slots]
                packed[to_img * wide + half * some + brick] = jnp.concatenate(
                    [block[:, :lanes], block[:, lanes:]], axis=0
                ).astype(jnp.bfloat16)
            return 0

        lax.fori_loop(0, 2, pack, 0)

        def inner(df, _):
            to_freq = (freq + df) % wide

            @pl.when((di > 0) | (df > 0))
            def _():
                pltpu.make_async_remote_copy(
                    src_ref=packed.at[to_img * wide + to_freq],
                    dst_ref=arrived.at[me],
                    send_sem=send_sem,
                    recv_sem=recv_sem.at[di],
                    device_id={"img": to_img, "freq": to_freq},
                    device_id_type=MESH,
                ).start()

            return 0

        lax.fori_loop(0, wide, inner, 0)

    def take_group(turn):
        di = order[turn]
        group = (img + groups - di) % groups
        count = wide - 1 if di == 0 else wide
        some = pl.ds(0, count)
        pltpu.make_async_copy(arrived.at[some], arrived.at[some], recv_sem.at[di]).wait()
        if di == 0:
            own = pltpu.make_async_copy(packed.at[me], arrived.at[me], own_sem)
            own.start()
            own.wait()
        for pair in range(wide // 2):
            blocks = [
                arrived[group * wide + 2 * pair + n].astype(jnp.float32) for n in range(2)
            ]
            for part in range(2):
                both = [block[part * slots : (part + 1) * slots] for block in blocks]
                terms[2 * pair * slots : 2 * (pair + 1) * slots, part * lanes : (part + 1) * lanes] = (
                    jnp.concatenate(both, axis=0).astype(jnp.bfloat16)
                )

        for here in (slice(0, row_step), slice(row_step, BROWS)):
            found = jnp.dot(
                members[turn % held, here, :], terms[...], preferred_element_type=jnp.float32
            )
            if turn > 0:
                found = found + jnp.concatenate([out_ref[0, 0, here, :], out_ref[0, 1, here, :]], axis=1)
            out_ref[0, 0, here, :] = found[:, :lanes]
            out_ref[0, 1, here, :] = found[:, lanes:]
        if turn + held < groups:
            make_members(turn + held)

    for turn in range(groups + 8):
        if turn < groups:
            send_group(order[turn])
        if turn >= 8:
            take_group(turn - 8)
    pltpu.make_async_copy(packed.at[most], packed.at[most], send_sem).wait()


def back_projected(rounded, images, code_column, kernel_taps, places, table, image_groups):
    rows = rounded.shape[0] // image_groups
    parts, count, freqs = images.shape
    block = (parts, rows, freqs)
    bricks, segments, lanes = table.shape[0], places.shape[1], 128
    return pl.pallas_call(
        volume_kernel,
        out_shape=jax.ShapeDtypeStruct((1, parts, BROWS, lanes), jnp.float32),
        in_specs=[pl.BlockSpec(memory_space=VMEM)] * 2
        + [pl.BlockSpec(memory_space=pltpu.SMEM)]
        + [pl.BlockSpec(memory_space=VMEM)] * 2
        + [pl.BlockSpec(memory_space=pl.ANY)],
        out_specs=pl.BlockSpec(memory_space=VMEM),
        scratch_shapes=[
            VMEM(images.shape, jnp.bfloat16),
            VMEM((2 * rows, count), jnp.bfloat16),
            VMEM((image_groups, *block), jnp.bfloat16),
            VMEM(block, jnp.bfloat16),
            VMEM((2, *block), jnp.bfloat16),
            VMEM(block, jnp.bfloat16),
            VMEM((2, *block), jnp.bfloat16),
            VMEM(block, jnp.bfloat16),
            VMEM((2, MOVED, freqs), jnp.bfloat16),
            VMEM(block, jnp.float32),
            VMEM((segments, 2 * lanes), jnp.bfloat16),
            VMEM((bricks, 2 * SLOTS, lanes), jnp.bfloat16),
            VMEM((bricks, 2 * SLOTS, lanes), jnp.bfloat16),
            VMEM((bricks, 1, 128), jnp.int32),
            VMEM((4, BROWS, 16 * SLOTS), jnp.bfloat16),
            VMEM((16 * SLOTS, 2 * lanes), jnp.bfloat16),
            VMEM((segments // rows, rows, kernel_taps.shape[1]), jnp.float32),
            DMA((2,)),
            DMA((16,)),
            DMA((16,)),
            DMA(()),
            DMA((8,)),
            DMA(()),
            DMA(()),
            DMA(()),
        ],
        compiler_params=pltpu.CompilerParams(
            collective_id=2, has_side_effects=True, vmem_limit_bytes=VMEM_BYTES
        ),
    )(rounded, code_column, kernel_taps, places, table, images)


def on_device(
    images,
    references,
    noise_weight,
    prior_orient,
    segment_brick,
    segment_row,
    segment_kernel,
    kernel_taps,
):
    image_groups = lax.axis_size("img")
    freq_groups = lax.axis_size("freq")
    local_orients = references.shape[1]
    segment_blocks = segment_row.shape[2]
    codes = (segment_brick[..., 0] << BRICK_SHIFT) + (segment_row << ROW_SHIFT) + segment_kernel
    codes = codes.reshape(local_orients, segment_blocks).T.reshape(-1)
    code_row = jnp.concatenate([codes, prior_orient])[None, :]
    code_column = codes[:, None]
    rounded, own_rows, places, table = posteriors(
        references, noise_weight, code_row, code_column, images, image_groups, freq_groups
    )
    volume = back_projected(
        rounded, images, code_column, kernel_taps, places, table, image_groups
    )
    return (own_rows, volume)


def solution(mesh):
    in_specs = (
        P(None, "img", "freq"),
        P(None, "img", "freq"),
        P("freq"),
        P("img"),
        P("freq", "img", None, None),
        P("freq", "img", None),
        P("freq", "img", None),
        P(),
    )
    out_specs = (P("freq", "img"), P(("img", "freq"), None, None, None))
    return jax.shard_map(
        on_device, mesh=mesh, in_specs=in_specs, out_specs=out_specs, check_vma=False
    )
```

```python
import jax
import jax.numpy as jnp
from jax import lax
from jax.experimental import pallas as pl
from jax.experimental.pallas import tpu as pltpu
from jax.sharding import PartitionSpec as P

MESH = pl.DeviceIdType.MESH
VMEM = pltpu.VMEM
DMA = pltpu.SemaphoreType.DMA
VMEM_BYTES = 60 * 1024 * 1024
RING = 4

BROWS = 2000
KEPT = 256
SLOTS = 40
MOVED = 32
ROW_SHIFT = 3
BRICK_SHIFT = 14
COARSE = 128
FINE = (64, 32, 16, 8)


tempering = 0.5
masked_logit = -1e30
contract_last = (((1,), (1,)), ((), ()))


def window_parts(prior_orient, orient_count):
    start = (prior_orient - orient_count // 8) % orient_count
    return start // COARSE, start % COARSE


def img_neighbours():
    me = lax.axis_index("img")
    z, x = me // RING, me % RING
    at = lambda other, shift: (z + other) % 2 * RING + (x + shift) % RING
    return at


def greet(others):
    barrier = pltpu.get_barrier_semaphore()
    for axis, other in others:
        pl.semaphore_signal(barrier, inc=1, device_id={axis: other}, device_id_type=MESH)
    pl.semaphore_wait(barrier, len(others))


def slot_tables(code_row, code_column, place_ref, lines, table_ref):
    segments = code_column.shape[0]
    bricks, step = table_ref.shape[0], 64
    named = jnp.right_shift(code_row[:, :segments], BRICK_SHIFT)
    ahead = lax.broadcasted_iota(jnp.int32, (1, segments), 1)

    def count_before(turn, rank):
        here = pl.ds(pl.multiple_of(turn * step, step), step)
        index = turn * step + lax.broadcasted_iota(jnp.int32, (step, 1), 0)
        same = (jnp.right_shift(code_column[here, :], BRICK_SHIFT) == named) & (index < ahead)
        return rank + jnp.sum(jnp.where(same, 1, 0), axis=0, keepdims=True)

    rank = lax.fori_loop(
        0, segments // step, count_before, jnp.zeros((1, segments), jnp.int32)
    )
    place_ref[...] = named * SLOTS + rank
    voxel = jnp.right_shift(code_row[:, :segments] & ((1 << BRICK_SHIFT) - 1), ROW_SHIFT)
    high = jnp.right_shift(voxel, 4)
    low = voxel - high * 16
    line = lax.broadcasted_iota(jnp.int32, (bricks, 1), 0)
    of_rank = jnp.where(rank == line, 1.0, 0.0).astype(jnp.bfloat16)
    table = jnp.zeros((bricks, 128), jnp.float32)
    for scale, digits in ((16.0, high), (1.0, low)):
        of_brick = jnp.where(named == line, digits.astype(jnp.float32), 0.0).astype(jnp.bfloat16)
        table = table + scale * lax.dot_general(
            of_brick, of_rank, contract_last, preferred_element_type=jnp.float32
        )
    lines[...] = table.astype(jnp.int32)

    def copy_line(brick, _):
        table_ref[brick] = lines[pl.ds(brick, 1), :]
        return 0

    lax.fori_loop(0, bricks, copy_line, 0)


def to_windows(scores_ref, prior_ref, windows_ref):
    orient_count = scores_ref.shape[0]

    def body(step, _):
        column = pl.ds(pl.multiple_of(step * 128, 128), 128)
        coarse, fine = window_parts(prior_ref[:, column], orient_count)
        rows = KEPT + sum(FINE)
        kept = scores_ref[:rows, column]
        for block in range(1, orient_count // COARSE):
            first = block * COARSE
            piece = scores_ref[first : min(first + rows, orient_count), column]
            if first + rows > orient_count:
                wrapped = scores_ref[: first + rows - orient_count, column]
                piece = jnp.concatenate([piece, wrapped], axis=0)
            kept = jnp.where(coarse == block, piece, kept)
        for size in FINE:
            rows -= size
            kept = jnp.where(fine // size % 2 == 1, kept[size : size + rows], kept[:rows])
        position = lax.broadcasted_iota(jnp.int32, (KEPT, 1), 0) - fine % FINE[-1]
        inside = (position >= 0) & (position <= 2 * (orient_count // 8))
        windows_ref[column, :] = jnp.where(inside, kept, masked_logit).T
        return 0

    lax.fori_loop(0, scores_ref.shape[1] // 128, body, 0)


def from_windows(kept_ref, prior_ref, wide_ref, rounded_ref):
    orient_count = wide_ref.shape[0]

    def body(step, _):
        column = pl.ds(pl.multiple_of(step * 128, 128), 128)
        coarse, fine = window_parts(prior_ref[:, column], orient_count)
        kept = kept_ref[column, :].astype(jnp.float32).T
        for size in FINE[::-1]:
            pad = jnp.zeros((size, 128), jnp.float32)
            kept = jnp.where(
                fine // size % 2 == 1,
                jnp.concatenate([pad, kept], axis=0),
                jnp.concatenate([kept, pad], axis=0),
            )
        kept = jnp.concatenate([kept, jnp.zeros((-kept.shape[0] % COARSE, 128), jnp.float32)], axis=0)
        blocks = orient_count // COARSE
        for block in range(blocks):
            part = jnp.zeros((COARSE, 128), jnp.float32)
            for piece in range(kept.shape[0] // COARSE):
                part = jnp.where(
                    coarse == (block - piece) % blocks,
                    kept[piece * COARSE : (piece + 1) * COARSE],
                    part,
                )
            here = slice(block * COARSE, (block + 1) * COARSE)
            wide_ref[here, column] = part
            rounded_ref[here, column] = part.astype(jnp.bfloat16)
        return 0

    lax.fori_loop(0, wide_ref.shape[1] // 128, body, 0)


def posterior_kernel(
    refs_ref, noise_ref, code_row, code_column, images_hbm,
    rounded_ref, rows_ref, place_ref, table_ref,
    images, gathered, weighted, energy, out_ref, windows_ref, kept_ref, lines,
    pair_in, chip_out, chip_in, load_sem, own_sem, send_sem, recv_sem,
    pair_send, pair_recv, chip_send, chip_recv, gat_send, gat_recv, sib_send, sib_recv,
):
    freq = lax.axis_index("freq")
    core = freq % 2
    z, y = freq // 8, freq // 2 % 4
    count = windows_ref.shape[0] // 16
    sibling = freq + 1 - 2 * core
    spots = [(dz, dy) for dz, dy in ((1, 2), (1, 1), (1, 3), (0, 2), (1, 0), (0, 1), (0, 3), (0, 0))]
    target = lambda dz, dy: (z + dz) % 2 * 8 + (y + dy) % 4 * 2 + core
    source = lambda dz, dy: (z + dz) % 2 * 8 + (y + 4 - dy) % 4 * 2 + core
    at = img_neighbours()
    rows = refs_ref.shape[1]
    load = pltpu.make_async_copy(images_hbm, images, load_sem)
    load.start()
    own = pltpu.make_async_copy(refs_ref, gathered.at[at(0, 0)], own_sem)
    own.start()
    greet(
        [("img", at(0, 1)), ("img", at(0, 3)), ("img", at(1, 0)), ("freq", sibling)]
        + [("freq", target(*spot)) for spot in spots[:-1]]
    )
    own.wait()

    def forward(number, shard, part, target, first=0, last=rows):
        some = gathered.at[shard, part, pl.ds(first, last - first)]
        copy = pltpu.make_async_remote_copy(
            src_ref=some,
            dst_ref=some,
            send_sem=send_sem.at[number],
            recv_sem=recv_sem.at[number],
            device_id={"img": target},
            device_id_type=MESH,
        )
        copy.start()
        return copy

    right, left, across = at(0, 1), at(0, 3), at(1, 0)
    mine = at(0, 0)
    own_right = [forward(0, mine, 0, right), None]
    own_left = [None, forward(1, mine, 1, left)]
    own_across = [forward(2, mine, 0, across), None]
    own_right[1] = forward(3, mine, 1, right)
    own_left[0] = forward(4, mine, 0, left)
    own_across[1] = forward(5, mine, 1, across)

    def weigh(shard, part, place, fresh, bank):
        lines = 16
        for first in range(0, rows, lines):
            value = gathered[shard, part, first : first + lines, :].astype(jnp.float32)
            scaled = value * noise_ref[...]
            here = slice(place * rows + first, place * rows + first + lines)
            weighted[here, :] = scaled.astype(jnp.bfloat16)
            squares = scaled * value
            total = squares[:, :128]
            for lane in range(128, squares.shape[1], 128):
                total = total + squares[:, lane : lane + 128]
            energy[bank, here, :] = total if fresh else energy[bank, here, :] + total

    def multiply(first, second, part, fresh, bank=0):
        weigh(first, part, 0, fresh, bank)
        weigh(second, part, 1, fresh, bank)
        if not fresh:
            half = 0.5 * jnp.sum(energy[bank], axis=1, keepdims=True)
        width = 256

        def body(step, _):
            column = pl.ds(pl.multiple_of(step * width, width), width)
            product = lax.dot_general(
                weighted[...], images[part, column, :], contract_last,
                preferred_element_type=jnp.float32,
            )
            if not fresh:
                product = product - half
            for place, shard in enumerate((first, second)):
                block = product[place * rows : (place + 1) * rows]
                there = pl.ds(pl.multiple_of(shard * rows, 16), rows)
                if fresh:
                    out_ref[there, column] = block
                else:
                    out_ref[there, column] = out_ref[there, column] + block
            return 0

        lax.fori_loop(0, images.shape[1] // width, body, 0)

    slot_tables(code_row, code_column, place_ref, lines, table_ref)
    own_right[0].wait_recv()
    next_right = forward(6, at(0, 3), 0, right)
    own_left[1].wait_recv()
    next_left = forward(7, at(0, 1), 1, left)
    extra = [forward(14, at(0, 1), 1, across, rows - MOVED), None]
    load.wait()
    own_across[0].wait_recv()
    over_right = [forward(8, at(1, 0), 0, right), None]
    over_left = [forward(9, at(1, 0), 0, left), None]
    multiply(at(0, 0), at(1, 0), 0, True)
    own_across[1].wait_recv()
    over_right[1] = forward(10, at(1, 0), 1, right, 0, rows - MOVED)
    over_left[1] = forward(11, at(1, 0), 1, left, 0, rows - MOVED)
    own_right[1].wait_recv()
    extra[1] = forward(15, at(0, 3), 1, across, rows - MOVED)
    multiply(at(0, 0), at(1, 0), 1, False)
    own_left[0].wait_recv()
    multiply(at(0, 1), at(0, 3), 0, True)
    multiply(at(0, 1), at(0, 3), 1, False)
    next_right.wait_recv()
    over_across = [forward(12, at(0, 2), 0, across), None]
    next_left.wait_recv()
    over_across[1] = forward(13, at(0, 2), 1, across)
    over_right[0].wait_recv()
    over_left[0].wait_recv()
    multiply(at(1, 1), at(1, 3), 0, True)
    over_across[0].wait_recv()
    multiply(at(0, 2), at(1, 2), 0, True, 1)
    for copy in (over_right[1], over_left[1], extra[0], extra[1]):
        copy.wait_recv()
    multiply(at(1, 1), at(1, 3), 1, False)
    over_across[1].wait_recv()
    multiply(at(0, 2), at(1, 2), 1, False, 1)
    for copy in (
        own_right + own_left + own_across + [next_right, next_left]
        + over_right + over_left + over_across + extra
    ):
        copy.wait_send()
    prior_ref = code_row.at[:, pl.ds(code_column.shape[0], out_ref.shape[1])]
    to_windows(out_ref, prior_ref, windows_ref)
    block_lines = lambda block: pl.ds(pl.multiple_of(block * count, 16), count)

    def send(src, dst, send_sem, recv_sem, other):
        copy = pltpu.make_async_remote_copy(
            src_ref=src, dst_ref=dst, send_sem=send_sem, recv_sem=recv_sem,
            device_id={"freq": other}, device_id_type=MESH,
        )
        copy.start()
        return copy

    pairs = []
    for n, spot in enumerate(spots):
        block = target(*spot) + 1 - 2 * core
        pairs.append(
            send(windows_ref.at[block_lines(block)], pair_in.at[n], pair_send.at[n], pair_recv.at[n], sibling)
        )
    chips = []
    for n, spot in enumerate(spots):
        pairs[n].wait_recv()
        total = windows_ref[block_lines(target(*spot)), :] + pair_in[n]
        if n == 7:
            break
        chip_out[n] = total
        chips.append(
            send(chip_out.at[n], chip_in.at[n], chip_send.at[n], chip_recv.at[n], target(*spot))
        )
    chip_out[7] = total
    scores = chip_out[7]
    for n in range(7):
        chips[6 - n].wait_recv()
        scores = scores + chip_in[6 - n]
    inside = scores > 0.5 * masked_logit
    logits = jnp.where(inside, tempering * scores, masked_logit)
    raised = jnp.where(inside, jnp.exp(logits - jnp.max(logits, axis=1, keepdims=True)), 0.0)
    result = raised / jnp.sum(raised, axis=1, keepdims=True)
    kept_ref[block_lines(freq), :] = result.astype(jnp.bfloat16)
    gathers, relays = [], []
    for n, spot in enumerate(spots[:-1]):
        here = kept_ref.at[block_lines(freq)]
        gathers.append(send(here, here, gat_send.at[n], gat_recv.at[n], target(*spot)))
    here = kept_ref.at[block_lines(freq)]
    relays.append(send(here, here, sib_send.at[7], sib_recv.at[7], sibling))
    for n in range(6, -1, -1):
        gathers[n].wait_recv()
        here = kept_ref.at[block_lines(source(*spots[n]))]
        relays.append(send(here, here, sib_send.at[n], sib_recv.at[n], sibling))
    for copy in relays:
        copy.wait_recv()
    for copy in pairs + chips + gathers + relays:
        copy.wait_send()
    from_windows(kept_ref, prior_ref, out_ref, rounded_ref)
    share = rows_ref.shape[0]
    rows_ref[...] = out_ref[pl.ds(pl.multiple_of(freq * share, 8), share), :]


def posteriors(
    references, noise_weight, code_row, code_column, images, image_groups, freq_groups
):
    parts, rows, freqs = references.shape
    count = images.shape[1]
    orients, segments = image_groups * rows, code_column.shape[0]
    bricks = image_groups * freq_groups
    share = count // freq_groups
    return pl.pallas_call(
        posterior_kernel,
        out_shape=(
            jax.ShapeDtypeStruct((orients, count), jnp.bfloat16),
            jax.ShapeDtypeStruct((orients * share // count, count), jnp.float32),
            jax.ShapeDtypeStruct((1, segments), jnp.int32),
            jax.ShapeDtypeStruct((bricks, 1, 128), jnp.int32),
        ),
        in_specs=[pl.BlockSpec(memory_space=VMEM)] * 4 + [pl.BlockSpec(memory_space=pl.ANY)],
        out_specs=[pl.BlockSpec(memory_space=VMEM)] * 4,
        scratch_shapes=[
            VMEM(images.shape, jnp.bfloat16),
            VMEM((image_groups, parts, rows, freqs), jnp.bfloat16),
            VMEM((2 * rows, freqs), jnp.bfloat16),
            VMEM((2, 2 * rows, 128), jnp.float32),
            VMEM((orients, count), jnp.float32),
            VMEM((count, KEPT), jnp.float32),
            VMEM((count, KEPT), jnp.bfloat16),
            VMEM((bricks, 128), jnp.int32),
        ]
        + [VMEM((8, share, KEPT), jnp.float32) for _ in range(3)]
        + [DMA(()), DMA(()), DMA((16,)), DMA((16,))]
        + [DMA((8,)) for _ in range(8)],
        compiler_params=pltpu.CompilerParams(
            collective_id=0, has_side_effects=True, vmem_limit_bytes=VMEM_BYTES
        ),
    )(references, noise_weight.reshape(1, freqs), code_row, code_column, images)


def volume_kernel(
    rounded_ref, code_column, taps_ref, place_ref, table_ref, images_hbm, out_ref,
    images, lhs, part, first_in, side_in, half_in, near_in, last_in, extra_in, sums_ref,
    values, packed, arrived, lines_in, members, terms, factor_ref,
    load_sem, group_send, group_recv, send_sem, recv_sem, line_send, line_recv, own_sem,
):
    groups, wide = 8, 16
    img, freq = lax.axis_index("img"), lax.axis_index("freq")
    barrier = pltpu.get_barrier_semaphore()
    at = img_neighbours()
    rows, freqs = sums_ref.shape[1:]
    loads = []
    for n in range(2):
        loads.append(pltpu.make_async_copy(images_hbm.at[n], images.at[n], load_sem.at[n]))
        loads[-1].start()
    right, left, across = at(0, 1), at(0, 3), at(1, 0)

    def everyone(visit):
        def outer(di, _):
            def inner(df, _):
                @pl.when((di > 0) | (df > 0))
                def _():
                    visit(di, (img + di) % groups, (freq + df) % wide)

                return 0

            return lax.fori_loop(0, wide, inner, 0)

        lax.fori_loop(0, groups, outer, 0)

    everyone(
        lambda di, to_img, to_freq: pl.semaphore_signal(
            barrier, inc=1, device_id={"img": to_img, "freq": to_freq}, device_id_type=MESH
        )
    )

    def multiply(first, second, n):
        for place, (other, shift) in enumerate((first, second)):
            there = pl.ds(pl.multiple_of(at(other, shift) * rows, 16), rows)
            lhs[place * rows : (place + 1) * rows, :] = rounded_ref[there, :]
        width = 256

        def body(step, _):
            column = pl.ds(pl.multiple_of(step * width, width), width)
            product = jnp.dot(
                lhs[...], images[n, :, column], preferred_element_type=jnp.float32
            ).astype(jnp.bfloat16)
            for place, (other, shift) in enumerate((first, second)):
                part[other * 4 + shift, n, :, column] = product[place * rows : (place + 1) * rows]
            return 0

        lax.fori_loop(0, freqs // width, body, 0)

    copies = []

    def send(src, dst, target):
        number = len(copies)
        copy = pltpu.make_async_remote_copy(
            src_ref=src, dst_ref=dst, send_sem=group_send.at[number], recv_sem=group_recv.at[number],
            device_id={"img": target}, device_id_type=MESH,
        )
        copy.start()
        copies.append(copy)
        return copy

    def combine(dst, sources, count=rows):
        lines = 16

        def body(step, _):
            here = pl.ds(pl.multiple_of(step * lines, lines), lines)
            total = sources[0][here, :].astype(jnp.float32)
            for source in sources[1:]:
                total = total + source[here, :].astype(jnp.float32)
            dst[here, :] = total.astype(dst.dtype)
            return 0

        lax.fori_loop(0, count // lines, body, 0)

    stay = rows - MOVED
    kept, moved = pl.ds(0, stay), pl.ds(stay, MOVED)
    first, sides, near, extra = [], [[], []], [[None, None], [None, None]], []
    for n in range(2):
        loads[n].wait()
        multiply((1, 1), (1, 3), n)
        if n == 0:
            pl.semaphore_wait(barrier, groups * wide - 1)
        some = pl.ds(0, rows) if n == 0 else kept
        for way, (here, there) in enumerate(((5, right), (7, left))):
            sides[way].append(send(part.at[here, n, some], side_in.at[way, n, some], there))
        multiply((1, 2), (0, 2), n)
        first.append(send(part.at[6, n], first_in.at[n], across))
    for way, here in enumerate((5, 7)):
        extra.append(send(part.at[here, 1, moved], extra_in.at[way], across))
    me = img * wide + freq

    def send_line(di, to_img, to_freq):
        pltpu.make_async_remote_copy(
            src_ref=table_ref.at[to_img * wide + to_freq],
            dst_ref=lines_in.at[me],
            send_sem=line_send,
            recv_sem=line_recv,
            device_id={"img": to_img, "freq": to_freq},
            device_id_type=MESH,
        ).start()

    everyone(send_line)
    lines_in[me] = table_ref[me]

    for n in range(2):
        multiply((0, 1), (0, 3), n)
    halves = []
    first[0].wait_recv()
    combine(part.at[2, 0], [part.at[2, 0], first_in.at[0]])
    halves.append(send(part.at[2, 0], half_in.at[0], left))
    for n in range(2):
        multiply((1, 0), (0, 0), n)
    first[1].wait_recv()
    combine(part.at[2, 1], [part.at[2, 1], first_in.at[1]])
    halves.append(send(part.at[2, 1], half_in.at[1], right))
    near[0][0] = send(part.at[1, 0], near_in.at[0, 0], right)
    for way, here in enumerate((1, 3)):
        extra[way].wait_recv()
        some = part.at[here, 1, moved]
        combine(some, [some, extra_in.at[way]], MOVED)
    near[1][1] = send(part.at[3, 1], near_in.at[1, 1], left)
    phases, tap_count = taps_ref.shape
    for q in range(factor_ref.shape[0]):
        kernel = code_column[q * rows : (q + 1) * rows, :] & ((1 << ROW_SHIFT) - 1)
        for tap in range(tap_count):
            factor = jnp.zeros((rows, 1), jnp.float32)
            for phase in range(phases):
                factor = jnp.where(kernel == phase, taps_ref[phase, tap], factor)
            factor_ref[q, :, tap : tap + 1] = factor
    last = []
    for n in range(2):
        sides[0][n].wait_recv()
        sides[1][n].wait_recv()
        combine(
            part.at[4, n], [part.at[4, n], side_in.at[0, n], side_in.at[1, n]],
            rows if n == 0 else stay,
        )
        last.append(send(part.at[4, n], last_in.at[n], across))
    slots = packed.shape[1] // 2
    order = (0, 1, 2, 3, 4, 5, 6, 7)
    most = pl.ds(0, groups * wide - 1)
    place = lax.broadcasted_iota(jnp.int32, (1, 128), 1)
    chunks = wide * slots // 128
    row_step = 1008
    held = members.shape[0]

    def make_members(turn):
        group = (img + groups - order[turn]) % groups
        row_lines = [jnp.zeros((1, 128), jnp.int32) for _ in range(chunks)]
        for member in range(wide):
            line = lines_in[group * wide + member]
            chunk, first = member * slots // 128, member * slots % 128
            turned = pltpu.roll(line, first, 1) if first else line
            row_lines[chunk] = jnp.where(
                (place >= first) & (place < first + slots), turned, row_lines[chunk]
            )
            if first + slots > 128:
                row_lines[chunk + 1] = jnp.where(
                    place < first + slots - 128, turned, row_lines[chunk + 1]
                )
        row_lines = jnp.concatenate(row_lines, axis=1)

        def fill(step, _):
            first = pl.multiple_of(step * 16, 16)
            voxel = first + lax.broadcasted_iota(jnp.int32, (16, 1), 0)
            members[turn % held, pl.ds(first, 16), :] = jnp.where(row_lines == voxel, 1.0, 0.0).astype(
                jnp.bfloat16
            )
            return 0

        lax.fori_loop(0, BROWS // 16, fill, 0)

    pltpu.make_async_copy(lines_in.at[most], lines_in.at[most], line_recv).wait()
    pltpu.make_async_copy(table_ref.at[most], table_ref.at[most], line_send).wait()
    for turn in range(held):
        make_members(turn)
    halves[0].wait_recv()
    combine(part.at[3, 0], [part.at[3, 0], half_in.at[0]])
    near[1][0] = send(part.at[3, 0], near_in.at[1, 0], left)
    halves[1].wait_recv()
    combine(part.at[1, 1], [part.at[1, 1], half_in.at[1]])
    near[0][1] = send(part.at[1, 1], near_in.at[0, 1], right)
    segments = values.shape[0]
    lanes = freqs // (segments // rows)
    lane = lax.broadcasted_iota(jnp.int32, (rows, lanes), 1)

    def spread(part):
        for q in range(segments // rows):
            value = sums_ref[part, :, q * lanes : (q + 1) * lanes]
            shifted = [
                jnp.where(lane < lanes - 1, pltpu.roll(value, lanes - 1, 1), 0.0),
                value,
                jnp.where(lane >= 1, pltpu.roll(value, 1, 1), 0.0),
                jnp.where(lane >= 2, pltpu.roll(value, 2, 1), 0.0),
            ]
            result = factor_ref[q, :, 0:1] * shifted[0]
            for tap in range(1, 4):
                result = result + factor_ref[q, :, tap : tap + 1] * shifted[tap]
            values[q * rows : (q + 1) * rows, part * lanes : (part + 1) * lanes] = result.astype(
                jnp.bfloat16
            )

    for n in range(2):
        near[0][n].wait_recv()
        near[1][n].wait_recv()
        last[n].wait_recv()
        combine(
            sums_ref.at[n], [part.at[0, n], near_in.at[0, n], near_in.at[1, n], last_in.at[n]]
        )
        spread(n)
    for copy in copies:
        copy.wait_send()
    def send_group(di):
        to_img = (img + di) % groups
        some = wide // 2

        def pack(half, _):
            base = (to_img * wide + half * some) * slots
            slot = base + lax.broadcasted_iota(jnp.int32, (some * slots, 1), 0)
            found = jnp.zeros((some * slots, 2 * lanes), jnp.float32)
            step = 256
            for first in range(0, segments, step):
                hit = jnp.where(place_ref[:, first : first + step] == slot, 1.0, 0.0)
                found = found + jnp.dot(
                    hit.astype(jnp.bfloat16), values[first : first + step, :],
                    preferred_element_type=jnp.float32,
                )
            for brick in range(some):
                block = found[brick * slots : (brick + 1) * slots]
                packed[to_img * wide + half * some + brick] = jnp.concatenate(
                    [block[:, :lanes], block[:, lanes:]], axis=0
                ).astype(jnp.bfloat16)
            return 0

        lax.fori_loop(0, 2, pack, 0)

        def inner(df, _):
            to_freq = (freq + df) % wide

            @pl.when((di > 0) | (df > 0))
            def _():
                pltpu.make_async_remote_copy(
                    src_ref=packed.at[to_img * wide + to_freq],
                    dst_ref=arrived.at[me],
                    send_sem=send_sem,
                    recv_sem=recv_sem.at[di],
                    device_id={"img": to_img, "freq": to_freq},
                    device_id_type=MESH,
                ).start()

            return 0

        lax.fori_loop(0, wide, inner, 0)

    def take_group(turn):
        di = order[turn]
        group = (img + groups - di) % groups
        count = wide - 1 if di == 0 else wide
        some = pl.ds(0, count)
        pltpu.make_async_copy(arrived.at[some], arrived.at[some], recv_sem.at[di]).wait()
        if di == 0:
            own = pltpu.make_async_copy(packed.at[me], arrived.at[me], own_sem)
            own.start()
            own.wait()
        for pair in range(wide // 2):
            blocks = [
                arrived[group * wide + 2 * pair + n].astype(jnp.float32) for n in range(2)
            ]
            for part in range(2):
                both = [block[part * slots : (part + 1) * slots] for block in blocks]
                terms[2 * pair * slots : 2 * (pair + 1) * slots, part * lanes : (part + 1) * lanes] = (
                    jnp.concatenate(both, axis=0).astype(jnp.bfloat16)
                )

        for here in (slice(0, row_step), slice(row_step, BROWS)):
            found = jnp.dot(
                members[turn % held, here, :], terms[...], preferred_element_type=jnp.float32
            )
            if turn > 0:
                found = found + jnp.concatenate([out_ref[0, 0, here, :], out_ref[0, 1, here, :]], axis=1)
            out_ref[0, 0, here, :] = found[:, :lanes]
            out_ref[0, 1, here, :] = found[:, lanes:]
        if turn + held < groups:
            make_members(turn + held)

    for turn in range(groups + 8):
        if turn < groups:
            send_group(order[turn])
        if turn >= 8:
            take_group(turn - 8)
    pltpu.make_async_copy(packed.at[most], packed.at[most], send_sem).wait()


def back_projected(rounded, images, code_column, kernel_taps, places, table, image_groups):
    rows = rounded.shape[0] // image_groups
    parts, count, freqs = images.shape
    block = (parts, rows, freqs)
    bricks, segments, lanes = table.shape[0], places.shape[1], 128
    return pl.pallas_call(
        volume_kernel,
        out_shape=jax.ShapeDtypeStruct((1, parts, BROWS, lanes), jnp.float32),
        in_specs=[pl.BlockSpec(memory_space=VMEM)] * 2
        + [pl.BlockSpec(memory_space=pltpu.SMEM)]
        + [pl.BlockSpec(memory_space=VMEM)] * 2
        + [pl.BlockSpec(memory_space=pl.ANY)],
        out_specs=pl.BlockSpec(memory_space=VMEM),
        scratch_shapes=[
            VMEM(images.shape, jnp.bfloat16),
            VMEM((2 * rows, count), jnp.bfloat16),
            VMEM((image_groups, *block), jnp.bfloat16),
            VMEM(block, jnp.bfloat16),
            VMEM((2, *block), jnp.bfloat16),
            VMEM(block, jnp.bfloat16),
            VMEM((2, *block), jnp.bfloat16),
            VMEM(block, jnp.bfloat16),
            VMEM((2, MOVED, freqs), jnp.bfloat16),
            VMEM(block, jnp.float32),
            VMEM((segments, 2 * lanes), jnp.bfloat16),
            VMEM((bricks, 2 * SLOTS, lanes), jnp.bfloat16),
            VMEM((bricks, 2 * SLOTS, lanes), jnp.bfloat16),
            VMEM((bricks, 1, 128), jnp.int32),
            VMEM((4, BROWS, 16 * SLOTS), jnp.bfloat16),
            VMEM((16 * SLOTS, 2 * lanes), jnp.bfloat16),
            VMEM((segments // rows, rows, kernel_taps.shape[1]), jnp.float32),
            DMA((2,)),
            DMA((16,)),
            DMA((16,)),
            DMA(()),
            DMA((8,)),
            DMA(()),
            DMA(()),
            DMA(()),
        ],
        compiler_params=pltpu.CompilerParams(
            collective_id=2, has_side_effects=True, vmem_limit_bytes=VMEM_BYTES
        ),
    )(rounded, code_column, kernel_taps, places, table, images)


def on_device(
    images,
    references,
    noise_weight,
    prior_orient,
    segment_brick,
    segment_row,
    segment_kernel,
    kernel_taps,
):
    image_groups = lax.axis_size("img")
    freq_groups = lax.axis_size("freq")
    local_orients = references.shape[1]
    segment_blocks = segment_row.shape[2]
    codes = (segment_brick[..., 0] << BRICK_SHIFT) + (segment_row << ROW_SHIFT) + segment_kernel
    codes = codes.reshape(local_orients, segment_blocks).T.reshape(-1)
    code_row = jnp.concatenate([codes, prior_orient])[None, :]
    code_column = codes[:, None]
    rounded, own_rows, places, table = posteriors(
        references, noise_weight, code_row, code_column, images, image_groups, freq_groups
    )
    volume = back_projected(
        rounded, images, code_column, kernel_taps, places, table, image_groups
    )
    return (own_rows, volume)


def solution(mesh):
    in_specs = (
        P(None, "img", "freq"),
        P(None, "img", "freq"),
        P("freq"),
        P("img"),
        P("freq", "img", None, None),
        P("freq", "img", None),
        P("freq", "img", None),
        P(),
    )
    out_specs = (P("freq", "img"), P(("img", "freq"), None, None, None))
    return jax.shard_map(
        on_device, mesh=mesh, in_specs=in_specs, out_specs=out_specs, check_vma=False
    )
```
